512 devices in a mesh: lat: 64 (over z, y), row: 8 (over x, core).
Axes of the slice: x: 4, y: 4, z: 16, core: 2. Of those that a mesh axis runs over, the one named last changes fastest.
Arguments:
- store: bfloat16 [384, 4096], P('row'), may hold values from -6 to 6
- batch_rows: int32 [192], replicated, may hold values from 0 to 383
- bounds: int32 [5], replicated, may hold values from 1 to 64, as said below
- w_enc: bfloat16 [4096, 49152], P('row', 'lat'), may hold values from -0.09375 to 0.09375
- b_enc: float32 [49152], P('lat'), may hold values from -2.5 to -0.5
- w_dec: bfloat16 [49152, 4096], P('lat', 'row'), may hold values from -0.0546875 to 0.0546875
- b_dec: float32 [4096], P('row'), may hold values from -3 to 3
Outputs:
- grad_enc: bfloat16 [4096, 49152], P('row', 'lat')
- grad_benc: float32 [49152], P('lat')
- grad_dec: bfloat16 [49152, 4096], P('lat', 'row')
- grad_bdec: float32 [4096], P('row')
- losses: float32 [5], replicated
The draws below stay inside these ranges and needn't reach their ends.
Inputs may be any that keep to these rules, and one draw needn't show every extreme that they name: `bounds`: strictly increasing; the last equals 64; 32 and 33 are among them.
All inputs are finite; a program needn't handle non-finite values.
Results may differ from the reference program's by a relative error of at most 0.017.
Values may be sent and summed in bfloat16 or wider, within the bound.
A program may use at most 128 MiB of HBM per device.

```python
import jax
import jax.numpy as jnp
from jax import lax

D = 4096
LAT_DEV = 768
LATENTS = 49152
PREFIXES = 5
B = 192
STORE = 384
N_LAT = 64


def draw_bounds(key, part):
    key = jax.random.fold_in(key, 11)
    middle = N_LAT // 2
    picked = jax.random.permutation(key, N_LAT - 3)[:PREFIXES - 3].astype(jnp.int32) + 1
    picked = jnp.where(picked >= middle, picked + 2, picked)
    fixed_ends = jnp.array([middle, middle + 1], jnp.int32)
    ordered = jnp.sort(jnp.concatenate([picked, fixed_ends]))
    return jnp.concatenate([ordered, jnp.full((1,), N_LAT, jnp.int32)])


def set_ends(values, stream_key, least, high):
    dims = values.shape
    place = [jax.random.randint(jax.random.fold_in(stream_key, axis), (), 0, dims[axis]) for axis in range(len(dims))]
    values = values.at[tuple(place)].set(least)
    longest = dims.index(max(dims))
    place[longest] = (place[longest] + 1) % dims[longest]
    return values.at[tuple(place)].set(high)


def block_levels(stream_key, dims, cuts, smallest, largest):
    gain, own = 1.0, jax.random.fold_in(stream_key, 6)
    for dim, shards_of in cuts:
        steps = jnp.exp(jax.random.uniform(jax.random.fold_in(own, dim), (shards_of,), jnp.float32, smallest / len(cuts), largest / len(cuts)))
        gain = gain * jnp.repeat(steps, dims[dim] // shards_of).reshape([-1 if axis == dim else 1 for axis in range(len(dims))])
    return gain


def noise(own_key, shape, deviation, bound, shards=(), kind=jnp.bfloat16):
    factor_of = block_levels(own_key, shape, shards, -0.22, 0.18) if shards else 1.0
    values = jax.random.normal(own_key, shape, jnp.float32) * deviation * factor_of
    return jnp.minimum(jnp.maximum(values, -bound), bound).astype(kind)


def setup_inputs(seed: int = 0) -> dict:
    key_list = jax.random.split(jax.random.key(seed), 8)
    store = noise(key_list[0], (STORE, D), 1.0, 6.0, ((0, 8),))
    batch_rows = set_ends(jax.random.randint(key_list[1], (B,), 0, STORE), jax.random.fold_in(key_list[1], 1), 0, STORE - 1).astype(jnp.int32)
    bounds = draw_bounds(jax.random.fold_in(key_list[7], 71), 0)
    w_enc = noise(key_list[3], (D, LATENTS), D ** -0.5, 0.09375, ((0, 8), (1, 64)))
    b_enc = jnp.clip(-2.5 + 2.0 * jax.random.uniform(key_list[4], (LATENTS,), jnp.float32) ** block_levels(key_list[4], (LATENTS,), ((0, 64),), -0.2, 0.2), -2.5, -0.5)
    w_dec = noise(key_list[5], (LATENTS, D), (LATENTS // 4) ** -0.5, 0.0546875, ((0, 64), (1, 8)))
    b_dec = noise(key_list[6], (D,), 0.5, 3.0, ((0, 8),), jnp.float32)
    return dict(store=store, batch_rows=batch_rows, bounds=bounds, w_enc=w_enc, b_enc=b_enc, w_dec=w_dec, b_dec=b_dec)


def reference(store, batch_rows, bounds, w_enc, b_enc, w_dec, b_dec):
    batch_x = jnp.take(store, batch_rows, axis=0)
    target = batch_x.astype(jnp.float32) - b_dec
    centred = target.astype(jnp.bfloat16)
    preact = jnp.dot(centred, w_enc, preferred_element_type=jnp.float32) + b_enc
    codes = jax.nn.softplus(preact).astype(jnp.bfloat16)
    code_shards = codes.reshape(B, N_LAT, LAT_DEV).transpose(1, 0, 2)
    dec_shards = w_dec.reshape(N_LAT, LAT_DEV, D)
    shard_ids = jnp.arange(N_LAT, dtype=jnp.int32)

    def forward(carry, inputs_now):
        running, errors = carry
        shard, code_part, dec_part = inputs_now
        running = running + jnp.dot(code_part, dec_part, preferred_element_type=jnp.float32)
        is_end = bounds == shard + 1
        errors = jnp.where(is_end[:, None, None], (target - running)[None], errors)
        return (running, errors), None

    start = (jnp.zeros((B, D), jnp.float32), jnp.zeros((PREFIXES, B, D), jnp.float32))
    (running, errors), unused = lax.scan(forward, start, (shard_ids, code_shards, dec_shards))
    losses = jnp.sum(errors * errors, axis=(1, 2)) / (B * D)

    def backward(carry, inputs_now):
        shard, code_part, dec_part = inputs_now
        alive = (bounds > shard).astype(jnp.float32)
        suffix = jnp.sum(alive[:, None, None] * errors, axis=0)
        part_grad = (-2.0 / B * suffix).astype(jnp.bfloat16)
        dec_grad = lax.dot_general(code_part, part_grad, (((0,), (0,)), ((), ())), preferred_element_type=jnp.float32)
        code_grad = lax.dot_general(part_grad, dec_part, (((1,), (1,)), ((), ())), preferred_element_type=jnp.float32)
        return carry, (dec_grad.astype(jnp.bfloat16), code_grad)

    unused, (dec_grads, code_grads) = lax.scan(backward, jnp.zeros((), jnp.float32), (shard_ids, code_shards, dec_shards))
    grad_dec = dec_grads.reshape(LATENTS, D)
    code_grad = code_grads.transpose(1, 0, 2).reshape(B, LATENTS)
    pre_grad = code_grad * jax.nn.sigmoid(preact)
    grad_benc = jnp.sum(pre_grad, axis=0)
    grad_enc = jnp.dot(centred.T, pre_grad.astype(jnp.bfloat16), preferred_element_type=jnp.float32).astype(jnp.bfloat16)
    grad_bdec = -2.0 / B * jnp.sum(errors, axis=(0, 1)) - jnp.dot(w_enc.astype(jnp.float32), grad_benc, precision=lax.Precision.HIGHEST)
    return grad_enc, grad_benc, grad_dec, grad_bdec, losses
```

```python
import jax
import jax.numpy as jnp
from jax import lax
from jax.experimental import pallas as pl
from jax.experimental.pallas import tpu as pltpu
from jax.sharding import PartitionSpec as P

MESH = pl.DeviceIdType.MESH
BF16, F32 = jnp.bfloat16, jnp.float32

NX, NC, NY, NZ = 4, 2, 4, 16
ROWS = NX * NC
B, STORE, PREFIXES = 192, 384, 5
WIDTH, LAT = 512, 768
SB = STORE // ROWS
RB = B // NX
CB = LAT // NC
TILES = 12

X_ORDER = ((2, 0), (2, 1), (1, 0), (1, 1), (3, 0), (3, 1), (0, 1))
Z_ORDER = (8, 7, 9, 6, 10, 5, 11, 4, 12, 3, 13, 2, 14, 1, 15)
T_ORDER = (6, 5, 7, 4, 8, 3, 9, 2, 10, 1, 11, 0)

L_ENC, L_DEC, L_STORE, L_GDEC, L_GENC = range(5)
(S_STORE, S_PRE, S_CODES, S_PART, S_ZOUT, S_RET, S_GRAD, S_CODE, S_PG, S_SUM, S_LOSS, S_BY, S_BZ) = range(13)


def owner_z(t):
    return (t // 3) * 4 + lax.rem(t, 3)


def kernel(
    store, batch_rows, bounds, w_enc, b_enc, w_dec, b_dec,
    grad_enc, grad_benc, grad_dec, tail,
    wenc, wdec, cols, target, centred, pre_out, pre_in, sig, codes, part_out, ybuf, zout, zin, rout, rin,
    gout, pgrad, code_out, code_in, pgb, sums, lbuf, gdec, genc, by, bz,
    local_sem, send_sem, recv_sem, codes_sem, grad_sem,
):
    lat, row = lax.axis_index("lat"), lax.axis_index("row")
    z, y = lat // NY, lax.rem(lat, NY)
    x, c = row // NC, lax.rem(row, NC)

    def row_peers():
        for dx, dc in X_ORDER:
            yield lax.rem(x + dx, NX), lax.rem(c + dc, NC)

    def send(src, dst, sem, recv, lat_to, row_to):
        pltpu.make_async_remote_copy(
            src_ref=src, dst_ref=dst, send_sem=send_sem.at[sem], recv_sem=recv,
            device_id=(lat_to, row_to), device_id_type=MESH,
        ).start()

    def wait(ref, sem):
        pltpu.make_async_copy(ref, ref, sem).wait()

    def block(ref, xx, cc):
        return ref.at[pl.ds(pl.multiple_of(xx * RB, RB), RB), pl.ds(pl.multiple_of(cc * CB, CB), CB)]

    def band(ref, i):
        return ref.at[pl.ds(pl.multiple_of(i * RB, RB), RB)]

    get_enc = pltpu.make_async_copy(w_enc, wenc, local_sem.at[L_ENC])
    get_dec = pltpu.make_async_copy(w_dec, wdec, local_sem.at[L_DEC])
    own_cols = pl.ds(pl.multiple_of(row * WIDTH, WIDTH), WIDTH)
    own_slot = pl.ds(pl.multiple_of(row * SB, SB), SB)
    get_own = pltpu.make_async_copy(store.at[:, own_cols], cols.at[own_slot], local_sem.at[L_STORE])
    get_own.start()
    get_enc.start()
    get_dec.start()

    barrier = pltpu.get_barrier_semaphore()
    for xx, cc in row_peers():
        pl.semaphore_signal(barrier, inc=1, device_id=(lat, xx * NC + cc), device_id_type=MESH)
    for d in range(1, NY):
        pl.semaphore_signal(barrier, inc=1, device_id=(z * NY + lax.rem(y + d, NY), row), device_id_type=MESH)
    for d in Z_ORDER:
        pl.semaphore_signal(barrier, inc=1, device_id=(lax.rem(z + d, NZ) * NY + y, row), device_id_type=MESH)
    pl.semaphore_wait(barrier, ROWS - 1 + NY - 1 + NZ - 1)

    for xx, cc in row_peers():
        to = xx * NC + cc
        their_cols = pl.ds(pl.multiple_of(to * WIDTH, WIDTH), WIDTH)
        send(store.at[:, their_cols], cols.at[own_slot], S_STORE, recv_sem.at[S_STORE], lat, to)
    get_own.wait()
    wait(cols.at[pl.ds(0, SB * (ROWS - 1))], recv_sem.at[S_STORE])
    picks = (lax.broadcasted_iota(jnp.int32, (STORE, B), 0) == batch_rows[...]).astype(BF16)
    batch_x = lax.dot_general(picks, cols[...], (((0,), (0,)), ((), ())), preferred_element_type=F32)
    target[...] = batch_x - b_dec[...]
    centred[...] = target[...].astype(BF16)

    get_enc.wait()
    pre_out[...] = jnp.dot(centred[...], wenc[...], preferred_element_type=F32).astype(BF16)
    for xx, cc in row_peers():
        send(block(pre_out, xx, cc), pre_in.at[row], S_PRE, recv_sem.at[S_PRE], lat, xx * NC + cc)
    pre_in[row] = block(pre_out, x, c)[...]
    wait(pre_in.at[pl.ds(0, ROWS - 1)], recv_sem.at[S_PRE])
    preact = b_enc[:, pl.ds(pl.multiple_of(c * CB, CB), CB)] + pre_in[0].astype(F32)
    for r in range(1, ROWS):
        preact = preact + pre_in[r].astype(F32)
    small = jnp.exp(-jnp.abs(preact))
    log1p = jnp.where(small < 1e-3, small * (1.0 - 0.5 * small), jnp.log(1.0 + small))
    block(codes, x, c)[...] = (jnp.maximum(preact, 0.0) + log1p).astype(BF16)
    for xx, cc in row_peers():
        send(block(codes, x, c), block(codes, x, c), S_CODES, codes_sem.at[x], lat, xx * NC + cc)
    sig[...] = jnp.where(preact >= 0.0, 1.0, small) / (1.0 + small)

    get_dec.wait()
    for d in (0, 1, 3, 2):
        xx = lax.rem(x + d, NX)
        if d == 0:
            wait(block(codes, xx, 0), codes_sem.at[xx])
        else:
            wait(band(codes, xx), codes_sem.at[xx])
        part = jnp.dot(band(codes, xx)[...], wdec[...], preferred_element_type=F32).astype(BF16)
        band(part_out, xx)[...] = part

        @pl.when(xx != y)
        def _():
            send(band(part_out, xx), ybuf.at[y], S_PART, recv_sem.at[S_PART], z * NY + xx, row)

    ybuf[y] = band(part_out, y)[...]
    wait(ybuf.at[pl.ds(0, NY - 1)], recv_sem.at[S_PART])

    ends = [
        [jnp.where(bounds[k] == z * NY + j + 1, 1.0, 0.0).astype(F32) for k in range(PREFIXES)] for j in range(NY)
    ]
    ends_at = [sum(ends[j][1:], ends[j][0]) for j in range(NY)]
    total = ybuf[0].astype(F32)
    cut = ends_at[0] * total
    for j in range(1, NY):
        total = total + ybuf[j].astype(F32)
        cut = cut + ends_at[j] * total
    for t in range(TILES):
        i, k = divmod(t, 4)
        zout[t, 0] = total[16 * i : 16 * i + 16, 128 * k : 128 * k + 128].astype(BF16)
        zout[t, 1] = cut[16 * i : 16 * i + 16, 128 * k : 128 * k + 128].astype(BF16)
    is_owner = lax.rem(z, 4) < 3
    own_t = (z // 4) * 3 + jnp.minimum(lax.rem(z, 4), 2)
    for d in T_ORDER:
        t = lax.rem(own_t + d, TILES)
        to = owner_z(t)

        @pl.when(to != z)
        def _():
            send(zout.at[t], zin.at[z], S_ZOUT, recv_sem.at[S_ZOUT], to * NY + y, row)

    @pl.when(is_owner)
    def _():
        zin[z] = zout[own_t]
        rows = pl.ds(pl.multiple_of(y * RB + 16 * (own_t // 4), 16), 16)
        columns = pl.ds(pl.multiple_of(128 * lax.rem(own_t, 4), 128), 128)
        goal = target[rows, columns]
        wait(zin.at[pl.ds(0, NZ - 1)], recv_sem.at[S_ZOUT])
        below = jnp.zeros((16, 128), F32)
        errors = []
        for p in range(NZ):
            rout[p, 0] = below.astype(BF16)
            number = jnp.float32(0.0)
            for k in range(PREFIXES):
                inside = jnp.logical_and(bounds[k] > p * NY, bounds[k] <= (p + 1) * NY)
                number = number + jnp.where(inside, 1.0, 0.0).astype(F32)
            errors.append(number * (goal - below) - zin[p, 1].astype(F32))
            below = below + zin[p, 0].astype(F32)
        above = jnp.zeros((16, 128), F32)
        for p in range(NZ - 1, -1, -1):
            rout[p, 1] = above.astype(BF16)
            above = above + errors[p]
        for d in Z_ORDER:
            to = lax.rem(z + d, NZ)
            send(rout.at[to], rin.at[own_t], S_RET, recv_sem.at[S_RET], to * NY + y, row)
        rin[own_t] = rout[z]
        wait(rin.at[pl.ds(0, TILES - 1)], recv_sem.at[S_RET])

    @pl.when(jnp.logical_not(is_owner))
    def _():
        wait(rin, recv_sem.at[S_RET])

    def assemble(which):
        bands = [jnp.concatenate([rin[4 * i + k, which] for k in range(4)], axis=1) for i in range(3)]
        return jnp.concatenate(bands, axis=0).astype(F32)

    goal = band(target, y)[...] - assemble(0)
    suffix = assemble(1)
    inclusive = []
    running = ybuf[0].astype(F32)
    for j in range(NY):
        if j:
            running = running + ybuf[j].astype(F32)
        inclusive.append(goal - running)
    for j in range(NY - 1, -1, -1):
        suffix = suffix + ends_at[j] * inclusive[j]
        gout[j] = (-2.0 / B * suffix).astype(BF16)

        @pl.when(j != y)
        def _():
            send(gout.at[j], band(pgrad, y), S_GRAD, grad_sem.at[y], z * NY + j, row)

    band(pgrad, y)[...] = gout[y]

    for d in (0, 1, 3, 2):
        yy = lax.rem(y + d, NY)
        if d:
            wait(band(pgrad, yy), grad_sem.at[yy])
        partial = lax.dot_general(
            band(pgrad, yy)[...], wdec[...], (((1,), (1,)), ((), ())), preferred_element_type=F32
        )
        band(code_out, yy)[...] = partial.astype(BF16)
        for dc in range(NC):
            cc = lax.rem(c + dc, NC)
            to = yy * NC + cc

            @pl.when(to != row)
            def _():
                send(block(code_out, yy, cc), code_in.at[row], S_CODE, recv_sem.at[S_CODE], lat, to)

    code_in[row] = block(code_out, x, c)[...]

    lane = lax.broadcasted_iota(jnp.int32, (1, 128), 1)
    loss_row = jnp.zeros((1, 128), F32)
    ended = jnp.zeros((RB, WIDTH), F32)
    for j in range(NY):
        square = jnp.sum(inclusive[j] * inclusive[j], axis=0, keepdims=True)
        square = jnp.sum(square, axis=1, keepdims=True)
        mark = jnp.zeros((1, 128), F32)
        for k in range(PREFIXES):
            mark = mark + jnp.where(lane == k, ends[j][k], 0.0)
        loss_row = loss_row + square * mark
        ended = ended + ends_at[j] * inclusive[j]
    bias_row = -2.0 / B * jnp.sum(ended, axis=0, keepdims=True)
    lbuf[row] = jnp.broadcast_to(loss_row, (8, 128))
    for xx, cc in row_peers():
        send(lbuf.at[row], lbuf.at[row], S_LOSS, recv_sem.at[S_LOSS], lat, xx * NC + cc)

    gdec[...] = lax.dot_general(
        codes[...], pgrad[...], (((0,), (0,)), ((), ())), preferred_element_type=F32
    ).astype(BF16)
    put_dec = pltpu.make_async_copy(gdec, grad_dec, local_sem.at[L_GDEC])
    put_dec.start()

    wait(code_in.at[pl.ds(0, ROWS - 1)], recv_sem.at[S_CODE])
    code_grad = code_in[0].astype(F32)
    for r in range(1, ROWS):
        code_grad = code_grad + code_in[r].astype(F32)
    pre_grad = code_grad * sig[...]
    row_sum = pre_grad[0:8]
    for i in range(1, RB // 8):
        row_sum = row_sum + pre_grad[8 * i : 8 * i + 8]
    sums[row] = row_sum
    block(pgb, x, c)[...] = pre_grad.astype(BF16)
    for xx, cc in row_peers():
        send(sums.at[row], sums.at[row], S_SUM, recv_sem.at[S_SUM], lat, xx * NC + cc)
    for xx, cc in row_peers():
        send(block(pgb, x, c), block(pgb, x, c), S_PG, recv_sem.at[S_PG], lat, xx * NC + cc)

    wait(sums.at[pl.ds(0, ROWS - 1)], recv_sem.at[S_SUM])
    halves = []
    for cc in range(NC):
        half = sums[cc]
        for xx in range(1, NX):
            half = half + sums[xx * NC + cc]
        halves.append(jnp.sum(half, axis=0, keepdims=True))
    benc = jnp.concatenate(halves, axis=1)
    grad_benc[...] = benc
    high = benc.astype(BF16)
    middle = (benc - high.astype(F32)).astype(BF16)
    low = (benc - high.astype(F32) - middle.astype(F32)).astype(BF16)
    three = jnp.concatenate([high, middle, low, jnp.zeros((13, LAT), BF16)], axis=0)
    term = lax.dot_general(three, wenc[...], (((1,), (1,)), ((), ())), preferred_element_type=F32)
    bias_row = bias_row - (term[0:1] + (term[1:2] + term[2:3]))
    wait(lbuf.at[pl.ds(0, ROWS - 1)], recv_sem.at[S_LOSS])
    loss_all = lbuf[0, 0:1]
    for r in range(1, ROWS):
        loss_all = loss_all + lbuf[r, 0:1]
    pieces = [bias_row[:, 128 * k : 128 * k + 128] for k in range(4)]
    by[y] = jnp.concatenate(pieces + [loss_all, jnp.zeros((3, 128), F32)], axis=0)
    for d in range(1, NY):
        send(by.at[y], by.at[y], S_BY, recv_sem.at[S_BY], z * NY + lax.rem(y + d, NY), row)

    wait(code_in.at[pl.ds(0, ROWS - 1)], recv_sem.at[S_PG])
    genc[...] = lax.dot_general(
        centred[...], pgb[...], (((0,), (0,)), ((), ())), preferred_element_type=F32
    ).astype(BF16)
    put_enc = pltpu.make_async_copy(genc, grad_enc, local_sem.at[L_GENC])
    put_enc.start()

    wait(by.at[pl.ds(0, NY - 1)], recv_sem.at[S_BY])
    bz[z] = (by[0] + by[1]) + (by[2] + by[3])
    for d in Z_ORDER:
        to = lax.rem(z + d, NZ)
        send(bz.at[z], bz.at[z], S_BZ, recv_sem.at[S_BZ], to * NY + y, row)
    wait(bz.at[pl.ds(0, NZ - 1)], recv_sem.at[S_BZ])
    everything = bz[0]
    for p in range(1, NZ):
        everything = everything + bz[p]
    tail[...] = everything

    wait(cols.at[pl.ds(0, SB * (ROWS - 1))], send_sem.at[S_STORE])
    wait(pre_in.at[pl.ds(0, ROWS - 1)], send_sem.at[S_PRE])
    wait(pre_in.at[pl.ds(0, ROWS - 1)], send_sem.at[S_CODES])
    wait(ybuf.at[pl.ds(0, NY - 1)], send_sem.at[S_PART])

    @pl.when(is_owner)
    def _():
        wait(zout.at[pl.ds(0, TILES - 1)], send_sem.at[S_ZOUT])
        wait(rout.at[pl.ds(0, NZ - 1)], send_sem.at[S_RET])

    @pl.when(jnp.logical_not(is_owner))
    def _():
        wait(zout, send_sem.at[S_ZOUT])

    wait(gout.at[pl.ds(0, NY - 1)], send_sem.at[S_GRAD])
    wait(code_in.at[pl.ds(0, ROWS - 1)], send_sem.at[S_CODE])
    wait(code_in.at[pl.ds(0, ROWS - 1)], send_sem.at[S_PG])
    wait(sums.at[pl.ds(0, ROWS - 1)], send_sem.at[S_SUM])
    wait(lbuf.at[pl.ds(0, ROWS - 1)], send_sem.at[S_LOSS])
    wait(by.at[pl.ds(0, NY - 1)], send_sem.at[S_BY])
    wait(bz.at[pl.ds(0, NZ - 1)], send_sem.at[S_BZ])
    put_dec.wait()
    put_enc.wait()


def per_device(store, batch_rows, bounds, w_enc, b_enc, w_dec, b_dec):
    vmem, hbm = pl.BlockSpec(memory_space=pltpu.VMEM), pl.BlockSpec(memory_space=pl.ANY)
    smem = pl.BlockSpec(memory_space=pltpu.SMEM)
    grad_enc, grad_benc, grad_dec, tail = pl.pallas_call(
        kernel,
        out_shape=(
            jax.ShapeDtypeStruct((WIDTH, LAT), BF16),
            jax.ShapeDtypeStruct((1, LAT), F32),
            jax.ShapeDtypeStruct((LAT, WIDTH), BF16),
            jax.ShapeDtypeStruct((8, 128), F32),
        ),
        in_specs=[hbm, vmem, smem, hbm, vmem, hbm, vmem],
        out_specs=(hbm, vmem, hbm, vmem),
        scratch_shapes=[
            pltpu.VMEM((WIDTH, LAT), BF16),
            pltpu.VMEM((LAT, WIDTH), BF16),
            pltpu.VMEM((STORE, WIDTH), BF16),
            pltpu.VMEM((B, WIDTH), F32),
            pltpu.VMEM((B, WIDTH), BF16),
            pltpu.VMEM((B, LAT), BF16),
            pltpu.VMEM((ROWS, RB, CB), BF16),
            pltpu.VMEM((RB, CB), F32),
            pltpu.VMEM((B, LAT), BF16),
            pltpu.VMEM((B, WIDTH), BF16),
            pltpu.VMEM((NY, RB, WIDTH), BF16),
            pltpu.VMEM((TILES, 2, 16, 128), BF16),
            pltpu.VMEM((NZ, 2, 16, 128), BF16),
            pltpu.VMEM((NZ, 2, 16, 128), BF16),
            pltpu.VMEM((TILES, 2, 16, 128), BF16),
            pltpu.VMEM((NY, RB, WIDTH), BF16),
            pltpu.VMEM((B, WIDTH), BF16),
            pltpu.VMEM((B, LAT), BF16),
            pltpu.VMEM((ROWS, RB, CB), BF16),
            pltpu.VMEM((B, LAT), BF16),
            pltpu.VMEM((ROWS, 8, CB), F32),
            pltpu.VMEM((ROWS, 8, 128), F32),
            pltpu.VMEM((LAT, WIDTH), BF16),
            pltpu.VMEM((WIDTH, LAT), BF16),
            pltpu.VMEM((NY, 8, 128), F32),
            pltpu.VMEM((NZ, 8, 128), F32),
            pltpu.SemaphoreType.DMA((5,)),
            pltpu.SemaphoreType.DMA((13,)),
            pltpu.SemaphoreType.DMA((13,)),
            pltpu.SemaphoreType.DMA((NX,)),
            pltpu.SemaphoreType.DMA((NY,)),
        ],
        compiler_params=pltpu.CompilerParams(
            collective_id=0, has_side_effects=True, vmem_limit_bytes=40 * 2**20
        ),
        name="sae_step",
    )(store, batch_rows.reshape(1, B), bounds, w_enc, b_enc.reshape(1, LAT), w_dec, b_dec.reshape(1, WIDTH))
    return (
        grad_enc,
        grad_benc.reshape(LAT),
        grad_dec,
        tail[:4].reshape(WIDTH),
        tail[4, :PREFIXES] * (1.0 / (B * WIDTH * ROWS)),
    )


def solution(mesh):
    return jax.shard_map(
        per_device,
        mesh=mesh,
        in_specs=(P("row", None), P(), P(), P("row", "lat"), P("lat"), P("lat", "row"), P("row")),
        out_specs=(P("row", "lat"), P("lat"), P("lat", "row"), P("row"), P()),
        check_vma=False,
    )
```

```python
import jax
import jax.numpy as jnp
from jax import lax
from jax.experimental import pallas as pl
from jax.experimental.pallas import tpu as pltpu
from jax.sharding import PartitionSpec as P

MESH = pl.DeviceIdType.MESH
BF16, F32 = jnp.bfloat16, jnp.float32

NX, NC, NY, NZ = 4, 2, 4, 16
ROWS = NX * NC
B, STORE, PREFIXES = 192, 384, 5
WIDTH, LAT = 512, 768
SB = STORE // ROWS
GROUPS = 3
GR = B // GROUPS
RT = GR // NX
CB = LAT // NC
TILES = WIDTH // 128

X_ORDER = ((2, 0), (2, 1), (1, 0), (1, 1), (3, 0), (3, 1), (0, 1))
Z_ORDER = (8, 7, 9, 6, 10, 5, 11, 4, 12, 3, 13, 2, 14, 1, 15)
Y_ORDER = (2, 1, 3)

L_ENC, L_DEC, L_STORE, L_GDEC, L_GENC, L_ROWS, L_BENC, L_BDEC, L_BOUNDS = range(9)
S_PRE, S_CODES, S_PART, S_RET, S_GRAD, S_CODE = range(0, 18, 3)
S_STORE, S_ZOUT, S_PG, S_SUM, S_LOSS, S_BY, S_BZ = range(18, 25)


def kernel(
    store, batch_rows_hbm, bounds_hbm, w_enc, b_enc_hbm, w_dec, b_dec_hbm,
    grad_enc, grad_benc, grad_dec, tail,
    batch_rows, bounds, b_enc_flat, b_enc, b_dec, wenc, wdec, wenc_t, wdec_t, picks, cols, target, centred, pre_out, pre_in, sig, codes, part_out, ybuf, zout, zin, rout, rin,
    gout, pgrad, code_out, code_in, pgb, sums, lbuf, gdec, genc, by, bz,
    local_sem, send_sem, recv_sem, relay_sem,
):
    lat, row = lax.axis_index("lat"), lax.axis_index("row")
    z, y = lat // NY, lax.rem(lat, NY)
    x, c = row // NC, lax.rem(row, NC)

    def row_peers():
        for dx, dc in X_ORDER:
            yield lax.rem(x + dx, NX), lax.rem(c + dc, NC)

    def send(src, dst, sem, recv, lat_to, row_to):
        pltpu.make_async_remote_copy(
            src_ref=src, dst_ref=dst, send_sem=send_sem.at[sem], recv_sem=recv,
            device_id=(lat_to, row_to), device_id_type=MESH,
        ).start()

    def wait(ref, sem):
        pltpu.make_async_copy(ref, ref, sem).wait()

    def group(g):
        return pl.ds(g * GR, GR)

    def band(ref, g, i):
        return ref.at[pl.ds(pl.multiple_of(g * GR + i * RT, RT), RT)]

    def block(ref, g, xx, cc):
        return band(ref, g, xx).at[:, pl.ds(pl.multiple_of(cc * CB, CB), CB)]

    get_enc = pltpu.make_async_copy(w_enc, wenc, local_sem.at[L_ENC])
    get_dec = pltpu.make_async_copy(w_dec, wdec, local_sem.at[L_DEC])
    own_cols = pl.ds(pl.multiple_of(row * WIDTH, WIDTH), WIDTH)
    own_slot = pl.ds(pl.multiple_of(row * SB, SB), SB)
    get_own = pltpu.make_async_copy(store.at[:, own_cols], cols.at[own_slot], local_sem.at[L_STORE])
    get_rows = pltpu.make_async_copy(batch_rows_hbm, batch_rows, local_sem.at[L_ROWS])
    get_benc = pltpu.make_async_copy(b_enc_hbm, b_enc_flat, local_sem.at[L_BENC])
    get_bdec = pltpu.make_async_copy(b_dec_hbm, b_dec, local_sem.at[L_BDEC])
    get_bounds = pltpu.make_async_copy(bounds_hbm, bounds, local_sem.at[L_BOUNDS])
    gets = (get_own, get_rows, get_bdec, get_enc, get_benc, get_dec, get_bounds)
    for get in gets:
        get.start()
    pending = []

    barrier = pltpu.get_barrier_semaphore()
    for xx, cc in row_peers():
        pl.semaphore_signal(barrier, inc=1, device_id=(lat, xx * NC + cc), device_id_type=MESH)
    for d in range(1, NY):
        pl.semaphore_signal(barrier, inc=1, device_id=(z * NY + lax.rem(y + d, NY), row), device_id_type=MESH)
    next_z, last_z = lax.rem(z + 1, NZ) * NY + y, lax.rem(z + NZ - 1, NZ) * NY + y
    for to in (next_z, last_z):
        pl.semaphore_signal(barrier, inc=1, device_id=(to, row), device_id_type=MESH)
    pl.semaphore_wait(barrier, ROWS - 1 + NY - 1 + 2)

    def pass_on():
        pl.semaphore_signal(relay_sem.at[0], inc=1, device_id=(next_z, row), device_id_type=MESH)
        pl.semaphore_signal(relay_sem.at[1], inc=1, device_id=(last_z, row), device_id_type=MESH)

    def relay(last=False):
        pl.semaphore_wait(relay_sem.at[0], 1)
        pl.semaphore_wait(relay_sem.at[1], 1)
        if not last:
            pass_on()

    pass_on()

    for xx, cc in row_peers():
        to = xx * NC + cc
        their_cols = pl.ds(pl.multiple_of(to * WIDTH, WIDTH), WIDTH)
        send(store.at[:, their_cols], cols.at[own_slot], S_STORE, recv_sem.at[S_STORE], lat, to)
    pending.append((cols.at[pl.ds(0, SB * (ROWS - 1))], S_STORE))
    for get in gets:
        get.wait()
    b_enc[...] = b_enc_flat[...].reshape(1, LAT)
    rows_down = jnp.broadcast_to(batch_rows[...], (128, B)).T
    lanes = lax.broadcasted_iota(jnp.int32, (B, 128), 1)
    for k in range(STORE // 128):
        picks[:, 128 * k : 128 * k + 128] = (lanes + 128 * k == rows_down).astype(BF16)
    relay()
    relay()
    relay()
    wait(cols.at[pl.ds(0, SB * (ROWS - 1))], recv_sem.at[S_STORE])
    for g in range(GROUPS):
        rows = group(g)
        goal = jnp.dot(picks[rows], cols[...], preferred_element_type=F32) - b_dec[...]
        target[rows] = goal
        centred[rows] = goal.astype(BF16)
        pre_out[rows] = jnp.dot(centred[rows], wenc[...], preferred_element_type=F32).astype(BF16)
        for xx, cc in row_peers():
            send(block(pre_out, g, xx, cc), pre_in.at[g, row], S_PRE, recv_sem.at[S_PRE + g], lat, xx * NC + cc)
    pending.append((pre_in.at[:, pl.ds(0, ROWS - 1)], S_PRE))
    relay()
    relay()
    wenc_t[...] = wenc[...].T
    my_b_enc = b_enc[:, pl.ds(pl.multiple_of(c * CB, CB), CB)]
    for g in range(GROUPS):
        pre_in[g, row] = block(pre_out, g, x, c)[...]
        wait(pre_in.at[g, pl.ds(0, ROWS - 1)], recv_sem.at[S_PRE + g])
        preact = my_b_enc + pre_in[g, 0].astype(F32)
        for r in range(1, ROWS):
            preact = preact + pre_in[g, r].astype(F32)
        small = jnp.exp(-jnp.abs(preact))
        log1p = jnp.where(small < 1e-3, small * (1.0 - 0.5 * small), jnp.log(1.0 + small))
        block(codes, g, x, c)[...] = (jnp.maximum(preact, 0.0) + log1p).astype(BF16)
        for xx, cc in row_peers():
            send(block(codes, g, x, c), block(codes, g, x, c), S_CODES, recv_sem.at[S_CODES + g], lat, xx * NC + cc)
        sig[g] = jnp.where(preact >= 0.0, 1.0, small) / (1.0 + small)
    pending.append((pre_in.at[:, pl.ds(0, ROWS - 1)], S_CODES))

    relay()
    relay(last=True)
    wdec_t[...] = wdec[...].T
    for g in range(GROUPS):
        wait(pre_in.at[g, pl.ds(0, ROWS - 1)], recv_sem.at[S_CODES + g])
        part_out[group(g)] = jnp.dot(codes[group(g)], wdec[...], preferred_element_type=F32).astype(BF16)
        for d in Y_ORDER:
            to = lax.rem(y + d, NY)
            send(band(part_out, g, to), ybuf.at[g, y], S_PART, recv_sem.at[S_PART + g], z * NY + to, row)
        ybuf[g, y] = band(part_out, g, y)[...]
    pending.append((ybuf.at[:, pl.ds(0, NY - 1)], S_PART))

    ends = [
        [jnp.where(bounds[k] == z * NY + j + 1, 1.0, 0.0).astype(F32) for k in range(PREFIXES)] for j in range(NY)
    ]
    ends_at = [sum(ends[j][1:], ends[j][0]) for j in range(NY)]
    number = []
    for p in range(NZ):
        inside = [jnp.logical_and(bounds[k] > p * NY, bounds[k] <= (p + 1) * NY) for k in range(PREFIXES)]
        counts = [jnp.where(one, 1.0, 0.0).astype(F32) for one in inside]
        number.append(sum(counts[1:], counts[0]))
    for g in range(GROUPS):
        wait(ybuf.at[g, pl.ds(0, NY - 1)], recv_sem.at[S_PART + g])
        total = ybuf[g, 0].astype(F32)
        cut = ends_at[0] * total
        for j in range(1, NY):
            total = total + ybuf[g, j].astype(F32)
            cut = cut + ends_at[j] * total
        for k in range(TILES):
            zout[g, k, 0] = total[:, 128 * k : 128 * k + 128].astype(BF16)
            zout[g, k, 1] = cut[:, 128 * k : 128 * k + 128].astype(BF16)
        for d in range(TILES):
            k = lax.rem(z // 4 + (2, 1, 3, 0)[d], TILES)
            to = 4 * k + g

            @pl.when(to != z)
            def _():
                send(zout.at[g, k], zin.at[z], S_ZOUT, recv_sem.at[S_ZOUT], to * NY + y, row)

    own_g, own_k = lax.rem(z, 4), z // 4
    is_owner = own_g < GROUPS

    @pl.when(is_owner)
    def _():
        zin[z] = zout[own_g, own_k]
        rows = pl.ds(pl.multiple_of(own_g * GR + y * RT, RT), RT)
        columns = pl.ds(pl.multiple_of(128 * own_k, 128), 128)
        goal = target[rows, columns]
        wait(zin.at[pl.ds(0, NZ - 1)], recv_sem.at[S_ZOUT])
        below = jnp.zeros((RT, 128), F32)
        errors = []
        for p in range(NZ):
            rout[p, 0] = below.astype(BF16)
            errors.append(number[p] * (goal - below) - zin[p, 1].astype(F32))
            below = below + zin[p, 0].astype(F32)
        above = jnp.zeros((RT, 128), F32)
        for p in range(NZ - 1, -1, -1):
            rout[p, 1] = above.astype(BF16)
            above = above + errors[p]
        for d in Z_ORDER:
            to = lax.rem(z + d, NZ)
            send(rout.at[to], rin.at[own_g, own_k], S_RET, recv_sem.at[S_RET + own_g], to * NY + y, row)
        rin[own_g, own_k] = rout[z]

    lane = lax.broadcasted_iota(jnp.int32, (1, 128), 1)
    squares = [jnp.zeros((RT, WIDTH), F32) for j in range(NY)]
    ended = jnp.zeros((RT, WIDTH), F32)
    for g in range(GROUPS):

        @pl.when(own_g == g)
        def _():
            wait(rin.at[g, pl.ds(0, TILES - 1)], recv_sem.at[S_RET + g])

        @pl.when(own_g != g)
        def _():
            wait(rin.at[g], recv_sem.at[S_RET + g])

        below = jnp.concatenate([rin[g, k, 0] for k in range(TILES)], axis=1).astype(F32)
        suffix = jnp.concatenate([rin[g, k, 1] for k in range(TILES)], axis=1).astype(F32)
        running = band(target, g, y)[...] - below
        inclusive = []
        for j in range(NY):
            running = running - ybuf[g, j].astype(F32)
            inclusive.append(running)
        for j in range(NY - 1, -1, -1):
            suffix = suffix + ends_at[j] * inclusive[j]
            gout[g, j] = (-2.0 / B * suffix).astype(BF16)
        for d in Y_ORDER:
            to = lax.rem(y + d, NY)
            send(gout.at[g, to], band(pgrad, g, y), S_GRAD, recv_sem.at[S_GRAD + g], z * NY + to, row)
        band(pgrad, g, y)[...] = gout[g, y]
        for j in range(NY):
            squares[j] = squares[j] + inclusive[j] * inclusive[j]
            ended = ended + ends_at[j] * inclusive[j]
    pending.append((gout.at[:, pl.ds(0, NY - 1)], S_GRAD))

    loss_row = jnp.zeros((1, 128), F32)
    for j in range(NY):
        square = jnp.sum(jnp.sum(squares[j], axis=0, keepdims=True), axis=1, keepdims=True)
        mark = jnp.zeros((1, 128), F32)
        for k in range(PREFIXES):
            mark = mark + jnp.where(lane == k, ends[j][k], 0.0)
        loss_row = loss_row + square * mark
    bias_row = -2.0 / B * jnp.sum(ended, axis=0, keepdims=True)
    lbuf[row] = jnp.broadcast_to(loss_row, (8, 128))
    for xx, cc in row_peers():
        send(lbuf.at[row], lbuf.at[row], S_LOSS, recv_sem.at[S_LOSS], lat, xx * NC + cc)
    pending.append((lbuf.at[pl.ds(0, ROWS - 1)], S_LOSS))

    for g in range(GROUPS):
        wait(gout.at[g, pl.ds(0, NY - 1)], recv_sem.at[S_GRAD + g])
        code_out[group(g)] = jnp.dot(pgrad[group(g)], wdec_t[...], preferred_element_type=F32).astype(BF16)
        for xx, cc in row_peers():
            send(block(code_out, g, xx, cc), code_in.at[g, row], S_CODE, recv_sem.at[S_CODE + g], lat, xx * NC + cc)
        code_in[g, row] = block(code_out, g, x, c)[...]
    pending.append((code_in.at[:, pl.ds(0, ROWS - 1)], S_CODE))

    gdec[...] = lax.dot_general(
        codes[...], pgrad[...], (((0,), (0,)), ((), ())), preferred_element_type=F32
    ).astype(BF16)
    put_dec = pltpu.make_async_copy(gdec, grad_dec, local_sem.at[L_GDEC])
    put_dec.start()

    row_sum = jnp.zeros((8, CB), F32)
    for g in range(GROUPS):
        wait(code_in.at[g, pl.ds(0, ROWS - 1)], recv_sem.at[S_CODE + g])
        code_grad = code_in[g, 0].astype(F32)
        for r in range(1, ROWS):
            code_grad = code_grad + code_in[g, r].astype(F32)
        pre_grad = code_grad * sig[g]
        row_sum = row_sum + (pre_grad[0:8] + pre_grad[8:16])
        block(pgb, g, x, c)[...] = pre_grad.astype(BF16)
    sums[row] = row_sum
    for xx, cc in row_peers():
        send(sums.at[row], sums.at[row], S_SUM, recv_sem.at[S_SUM], lat, xx * NC + cc)
    for g in range(GROUPS):
        for xx, cc in row_peers():
            send(block(pgb, g, x, c), block(pgb, g, x, c), S_PG, recv_sem.at[S_PG], lat, xx * NC + cc)
    pending.append((sums.at[pl.ds(0, ROWS - 1)], S_SUM))
    pending.append((code_in.at[:, pl.ds(0, ROWS - 1)], S_PG))

    wait(sums.at[pl.ds(0, ROWS - 1)], recv_sem.at[S_SUM])
    halves = []
    for cc in range(NC):
        half = sums[cc]
        for xx in range(1, NX):
            half = half + sums[xx * NC + cc]
        halves.append(jnp.sum(half, axis=0, keepdims=True))
    benc = jnp.concatenate(halves, axis=1)
    grad_benc[...] = benc
    high = benc.astype(BF16)
    middle = (benc - high.astype(F32)).astype(BF16)
    low = (benc - high.astype(F32) - middle.astype(F32)).astype(BF16)
    three = jnp.concatenate([high, middle, low, jnp.zeros((13, LAT), BF16)], axis=0)
    term = jnp.dot(three, wenc_t[...], preferred_element_type=F32)
    bias_row = bias_row - (term[0:1] + (term[1:2] + term[2:3]))
    wait(lbuf.at[pl.ds(0, ROWS - 1)], recv_sem.at[S_LOSS])
    loss_all = lbuf[0, 0:1]
    for r in range(1, ROWS):
        loss_all = loss_all + lbuf[r, 0:1]
    pieces = [bias_row[:, 128 * k : 128 * k + 128] for k in range(4)]
    by[y] = jnp.concatenate(pieces + [loss_all, jnp.zeros((3, 128), F32)], axis=0)
    for d in Y_ORDER:
        send(by.at[y], by.at[y], S_BY, recv_sem.at[S_BY], z * NY + lax.rem(y + d, NY), row)
    pending.append((by.at[pl.ds(0, NY - 1)], S_BY))

    wait(by.at[pl.ds(0, NY - 1)], recv_sem.at[S_BY])
    bz[z] = (by[0] + by[1]) + (by[2] + by[3])
    for d in Z_ORDER:
        to = lax.rem(z + d, NZ)
        send(bz.at[z], bz.at[z], S_BZ, recv_sem.at[S_BZ], to * NY + y, row)
    pending.append((bz.at[pl.ds(0, NZ - 1)], S_BZ))

    wait(code_in.at[:, pl.ds(0, ROWS - 1)], recv_sem.at[S_PG])
    genc[...] = lax.dot_general(
        centred[...], pgb[...], (((0,), (0,)), ((), ())), preferred_element_type=F32
    ).astype(BF16)
    put_enc = pltpu.make_async_copy(genc, grad_enc, local_sem.at[L_GENC])
    put_enc.start()

    @pl.when(is_owner)
    def _():
        wait(zin.at[pl.ds(0, GROUPS * TILES - 1)], send_sem.at[S_ZOUT])
        wait(rout.at[pl.ds(0, NZ - 1)], send_sem.at[S_RET])

    @pl.when(jnp.logical_not(is_owner))
    def _():
        wait(zin.at[pl.ds(0, GROUPS * TILES)], send_sem.at[S_ZOUT])

    for ref, sem in pending:
        wait(ref, send_sem.at[sem])
    put_dec.wait()
    put_enc.wait()
    wait(bz.at[pl.ds(0, NZ - 1)], recv_sem.at[S_BZ])
    everything = bz[0]
    for p in range(1, NZ):
        everything = everything + bz[p]
    tail[...] = everything


def finish(genc, benc, gdec, tail, grad_enc, grad_benc, grad_dec, grad_bdec, losses, sem):
    put_enc = pltpu.make_async_copy(genc, grad_enc, sem.at[0])
    put_dec = pltpu.make_async_copy(gdec, grad_dec, sem.at[1])
    put_enc.start()
    put_dec.start()
    grad_benc[...] = benc[...].reshape(LAT)
    grad_bdec[...] = tail[0:4].reshape(WIDTH)
    losses[...] = (tail[4] * (1.0 / (B * WIDTH * ROWS)))[0:PREFIXES]
    put_enc.wait()
    put_dec.wait()


def per_device(store, batch_rows, bounds, w_enc, b_enc, w_dec, b_dec):
    vmem, hbm = pl.BlockSpec(memory_space=pltpu.VMEM), pl.BlockSpec(memory_space=pl.ANY)
    operands = (store, batch_rows.reshape(1, B), bounds, w_enc, b_enc, w_dec, b_dec.reshape(1, WIDTH))
    genc, benc, gdec, tail = pl.pallas_call(
        kernel,
        out_shape=(
            jax.ShapeDtypeStruct((WIDTH, LAT), BF16),
            jax.ShapeDtypeStruct((1, LAT), F32),
            jax.ShapeDtypeStruct((LAT, WIDTH), BF16),
            jax.ShapeDtypeStruct((8, 128), F32),
        ),
        in_specs=[hbm] * 7,
        out_specs=(hbm, vmem, hbm, vmem),
        scratch_shapes=[
            pltpu.VMEM((1, B), jnp.int32),
            pltpu.SMEM((PREFIXES,), jnp.int32),
            pltpu.VMEM((LAT,), F32),
            pltpu.VMEM((1, LAT), F32),
            pltpu.VMEM((1, WIDTH), F32),
            pltpu.VMEM((WIDTH, LAT), BF16),
            pltpu.VMEM((LAT, WIDTH), BF16),
            pltpu.VMEM((LAT, WIDTH), BF16),
            pltpu.VMEM((WIDTH, LAT), BF16),
            pltpu.VMEM((B, STORE), BF16),
            pltpu.VMEM((STORE, WIDTH), BF16),
            pltpu.VMEM((B, WIDTH), F32),
            pltpu.VMEM((B, WIDTH), BF16),
            pltpu.VMEM((B, LAT), BF16),
            pltpu.VMEM((GROUPS, ROWS, RT, CB), BF16),
            pltpu.VMEM((GROUPS, RT, CB), F32),
            pltpu.VMEM((B, LAT), BF16),
            pltpu.VMEM((B, WIDTH), BF16),
            pltpu.VMEM((GROUPS, NY, RT, WIDTH), BF16),
            pltpu.VMEM((GROUPS, TILES, 2, RT, 128), BF16),
            pltpu.VMEM((NZ, 2, RT, 128), BF16),
            pltpu.VMEM((NZ, 2, RT, 128), BF16),
            pltpu.VMEM((GROUPS, TILES, 2, RT, 128), BF16),
            pltpu.VMEM((GROUPS, NY, RT, WIDTH), BF16),
            pltpu.VMEM((B, WIDTH), BF16),
            pltpu.VMEM((B, LAT), BF16),
            pltpu.VMEM((GROUPS, ROWS, RT, CB), BF16),
            pltpu.VMEM((B, LAT), BF16),
            pltpu.VMEM((ROWS, 8, CB), F32),
            pltpu.VMEM((ROWS, 8, 128), F32),
            pltpu.VMEM((LAT, WIDTH), BF16),
            pltpu.VMEM((WIDTH, LAT), BF16),
            pltpu.VMEM((NY, 8, 128), F32),
            pltpu.VMEM((NZ, 8, 128), F32),
            pltpu.SemaphoreType.DMA((9,)),
            pltpu.SemaphoreType.DMA((25,)),
            pltpu.SemaphoreType.DMA((25,)),
            pltpu.SemaphoreType.REGULAR((2,)),
        ],
        compiler_params=pltpu.CompilerParams(
            collective_id=0, has_side_effects=True, vmem_limit_bytes=40 * 2**20
        ),
        name="sae_step",
    )(*(pltpu.with_memory_space_constraint(operand, pltpu.HBM) for operand in operands))
    return pl.pallas_call(
        finish,
        out_shape=(
            jax.ShapeDtypeStruct((WIDTH, LAT), BF16),
            jax.ShapeDtypeStruct((LAT,), F32),
            jax.ShapeDtypeStruct((LAT, WIDTH), BF16),
            jax.ShapeDtypeStruct((WIDTH,), F32),
            jax.ShapeDtypeStruct((PREFIXES,), F32),
        ),
        in_specs=[hbm, vmem, hbm, vmem],
        out_specs=(hbm, vmem, hbm, vmem, vmem),
        scratch_shapes=[pltpu.SemaphoreType.DMA((2,))],
        compiler_params=pltpu.CompilerParams(vmem_limit_bytes=40 * 2**20),
        name="sae_finish",
    )(genc, benc, gdec, tail)


def solution(mesh):
    return jax.shard_map(
        per_device,
        mesh=mesh,
        in_specs=(P("row", None), P(), P(), P("row", "lat"), P("lat"), P("lat", "row"), P("row")),
        out_specs=(P("row", "lat"), P("lat"), P("lat", "row"), P("row"), P()),
        check_vma=False,
    )
```

```python
import jax
import jax.numpy as jnp
from jax import lax
from jax.experimental import pallas as pl
from jax.experimental.pallas import tpu as pltpu
from jax.sharding import PartitionSpec as P

MESH = pl.DeviceIdType.MESH
BF16, F32 = jnp.bfloat16, jnp.float32

NX, NC, NY, NZ = 4, 2, 4, 16
ROWS = NX * NC
B, STORE, PREFIXES = 192, 384, 5
WIDTH, LAT = 512, 768
SB = STORE // ROWS
GROUPS = 3
GR = B // GROUPS
RT = GR // NX
CB = LAT // NC
MEMBERS, CLUSTERS = 16, 4

X_ORDER = ((2, 0), (2, 1), (1, 0), (1, 1), (3, 0), (3, 1), (0, 1))
Z_ORDER = (8, 7, 9, 6, 10, 5, 11, 4, 12, 3, 13, 2, 14, 1, 15)
Y_ORDER = (2, 1, 3)

L_ENC, L_DEC, L_STORE, L_GDEC, L_GENC, L_ROWS, L_BENC, L_BDEC, L_BOUNDS = range(9)
S_PRE, S_CODES, S_PART, S_FAR, S_GRAD, S_CODE = range(0, 18, 3)
S_STORE, S_PG, S_SUM, S_BY, S_BZ = range(18, 23)


def kernel(
    store, batch_rows_hbm, bounds_hbm, w_enc, b_enc_hbm, w_dec, b_dec_hbm,
    grad_enc, grad_benc, grad_dec, tail,
    batch_rows, bounds, b_enc_flat, b_enc, b_dec, wenc, wdec, wenc_t, wdec_t, slope, picks, cols, target, centred, pre_out, pre_in, sig, codes, part_out, parts, far,
    grads, pgrad, code_out, code_in, pgb, sums, gdec, genc, by, bz,
    local_sem, send_sem, recv_sem, relay_sem,
):
    lat, row = lax.axis_index("lat"), lax.axis_index("row")
    z, y = lat // NY, lax.rem(lat, NY)
    cluster, member = lat // MEMBERS, lax.rem(lat, MEMBERS)
    x, c = row // NC, lax.rem(row, NC)

    def row_peers():
        for dx, dc in X_ORDER:
            yield lax.rem(x + dx, NX), lax.rem(c + dc, NC)

    def send(src, dst, sem, recv, lat_to, row_to):
        pltpu.make_async_remote_copy(
            src_ref=src, dst_ref=dst, send_sem=send_sem.at[sem], recv_sem=recv,
            device_id=(lat_to, row_to), device_id_type=MESH,
        ).start()

    def wait(ref, sem):
        pltpu.make_async_copy(ref, ref, sem).wait()

    def group(g):
        return pl.ds(g * GR, GR)

    def band(ref, g, i):
        return ref.at[pl.ds(pl.multiple_of(g * GR + i * RT, RT), RT)]

    def tile(ref, g, m):
        return band(ref, g, lax.rem(m, NY)).at[:, pl.ds(pl.multiple_of(m // NY * 128, 128), 128)]

    def block(ref, g, xx, cc):
        return band(ref, g, xx).at[:, pl.ds(pl.multiple_of(cc * CB, CB), CB)]

    get_enc = pltpu.make_async_copy(w_enc, wenc, local_sem.at[L_ENC])
    get_dec = pltpu.make_async_copy(w_dec, wdec, local_sem.at[L_DEC])
    own_cols = pl.ds(pl.multiple_of(row * WIDTH, WIDTH), WIDTH)
    own_slot = pl.ds(pl.multiple_of(row * SB, SB), SB)
    get_own = pltpu.make_async_copy(store.at[:, own_cols], cols.at[own_slot], local_sem.at[L_STORE])
    get_rows = pltpu.make_async_copy(batch_rows_hbm, batch_rows, local_sem.at[L_ROWS])
    get_benc = pltpu.make_async_copy(b_enc_hbm, b_enc_flat, local_sem.at[L_BENC])
    get_bdec = pltpu.make_async_copy(b_dec_hbm, b_dec, local_sem.at[L_BDEC])
    get_bounds = pltpu.make_async_copy(bounds_hbm, bounds, local_sem.at[L_BOUNDS])
    gets = (get_own, get_rows, get_bdec, get_enc, get_benc, get_dec, get_bounds)
    for get in gets:
        get.start()
    pending = []

    barrier = pltpu.get_barrier_semaphore()
    for xx, cc in row_peers():
        pl.semaphore_signal(barrier, inc=1, device_id=(lat, xx * NC + cc), device_id_type=MESH)
    for d in range(1, NY):
        pl.semaphore_signal(barrier, inc=1, device_id=(z * NY + lax.rem(y + d, NY), row), device_id_type=MESH)
    next_z, last_z = lax.rem(z + 1, NZ) * NY + y, lax.rem(z + NZ - 1, NZ) * NY + y
    for to in (next_z, last_z):
        pl.semaphore_signal(barrier, inc=1, device_id=(to, row), device_id_type=MESH)
    pl.semaphore_wait(barrier, ROWS - 1 + NY - 1 + 2)

    def pass_on():
        pl.semaphore_signal(relay_sem.at[0], inc=1, device_id=(next_z, row), device_id_type=MESH)
        pl.semaphore_signal(relay_sem.at[1], inc=1, device_id=(last_z, row), device_id_type=MESH)

    def relay(last=False):
        pl.semaphore_wait(relay_sem.at[0], 1)
        pl.semaphore_wait(relay_sem.at[1], 1)
        if not last:
            pass_on()

    pass_on()

    for xx, cc in row_peers():
        to = xx * NC + cc
        their_cols = pl.ds(pl.multiple_of(to * WIDTH, WIDTH), WIDTH)
        send(store.at[:, their_cols], cols.at[own_slot], S_STORE, recv_sem.at[S_STORE], lat, to)
    pending.append((cols.at[pl.ds(0, SB * (ROWS - 1))], S_STORE))
    for get in gets:
        get.wait()
    b_enc[...] = b_enc_flat[...].reshape(1, LAT)
    rows_down = jnp.broadcast_to(batch_rows[...], (128, B)).T
    lanes = lax.broadcasted_iota(jnp.int32, (B, 128), 1)
    for k in range(STORE // 128):
        picks[:, 128 * k : 128 * k + 128] = (lanes + 128 * k == rows_down).astype(BF16)
    relay()
    relay()
    relay()
    wait(cols.at[pl.ds(0, SB * (ROWS - 1))], recv_sem.at[S_STORE])
    for g in range(GROUPS):
        rows = group(g)
        goal = jnp.dot(picks[rows], cols[...], preferred_element_type=F32) - b_dec[...]
        target[rows] = goal
        centred[rows] = goal.astype(BF16)
        pre_out[rows] = jnp.dot(centred[rows], wenc[...], preferred_element_type=F32).astype(BF16)
        for xx, cc in row_peers():
            send(block(pre_out, g, xx, cc), pre_in.at[g, row], S_PRE, recv_sem.at[S_PRE + g], lat, xx * NC + cc)
    pending.append((pre_in.at[:, pl.ds(0, ROWS - 1)], S_PRE))
    relay()
    relay()
    my_b_enc = b_enc[:, pl.ds(pl.multiple_of(c * CB, CB), CB)]
    for g in range(GROUPS):
        pre_in[g, row] = block(pre_out, g, x, c)[...]
        wait(pre_in.at[g, pl.ds(0, ROWS - 1)], recv_sem.at[S_PRE + g])
        preact = my_b_enc + pre_in[g, 0].astype(F32)
        for r in range(1, ROWS):
            preact = preact + pre_in[g, r].astype(F32)
        small = jnp.exp(-jnp.abs(preact))
        log1p = jnp.where(small < 1e-3, small * (1.0 - 0.5 * small), jnp.log(1.0 + small))
        block(codes, g, x, c)[...] = (jnp.maximum(preact, 0.0) + log1p).astype(BF16)
        for xx, cc in row_peers():
            send(block(codes, g, x, c), block(codes, g, x, c), S_CODES, recv_sem.at[S_CODES + g], lat, xx * NC + cc)
        sig[g] = jnp.where(preact >= 0.0, 1.0, small) / (1.0 + small)
    pending.append((pre_in.at[:, pl.ds(0, ROWS - 1)], S_CODES))

    relay()
    relay(last=True)
    for g in range(GROUPS):
        wait(pre_in.at[g, pl.ds(0, ROWS - 1)], recv_sem.at[S_CODES + g])
        part_out[group(g)] = jnp.dot(codes[group(g)], wdec[...], preferred_element_type=F32).astype(BF16)
        for d in Z_ORDER:
            to = lax.rem(member + d, MEMBERS)
            send(
                tile(part_out, g, to), parts.at[g, member], S_PART, recv_sem.at[S_PART + g],
                cluster * MEMBERS + to, row,
            )
        parts[g, member] = tile(part_out, g, member)[...]
    pending.append((parts.at[:, pl.ds(0, MEMBERS - 1)], S_PART))

    soft = codes[...].astype(F32)
    slope[...] = jnp.where(soft < 0.01, soft * (1.0 - soft * (0.5 - soft * (1.0 / 6.0))), 1.0 - jnp.exp(-soft))
    wdec_t[...] = wdec[...].T
    wenc_t[...] = wenc[...].T

    ends = [
        [jnp.where(bounds[k] == cluster * MEMBERS + j + 1, 1.0, 0.0).astype(F32) for k in range(PREFIXES)]
        for j in range(MEMBERS)
    ]
    ends_at = [sum(ends[j][1:], ends[j][0]) for j in range(MEMBERS)]
    number, lower, higher = [], [], []
    for h in range(CLUSTERS):
        inside = [
            jnp.logical_and(bounds[k] > h * MEMBERS, bounds[k] <= (h + 1) * MEMBERS) for k in range(PREFIXES)
        ]
        counts = [jnp.where(one, 1.0, 0.0).astype(F32) for one in inside]
        number.append(sum(counts[1:], counts[0]))
        lower.append(jnp.where(h < cluster, 1.0, 0.0).astype(F32))
        higher.append(jnp.where(h > cluster, 1.0, 0.0).astype(F32))

    for g in range(GROUPS):
        wait(parts.at[g, pl.ds(0, MEMBERS - 1)], recv_sem.at[S_PART + g])
        total = parts[g, 0].astype(F32)
        cut = ends_at[0] * total
        for j in range(1, MEMBERS):
            total = total + parts[g, j].astype(F32)
            cut = cut + ends_at[j] * total
        far[g, cluster, 0] = total.astype(BF16)
        far[g, cluster, 1] = cut.astype(BF16)
        for d in (2, 1, 3):
            to = lax.rem(cluster + d, CLUSTERS) * MEMBERS + member
            send(far.at[g, cluster], far.at[g, cluster], S_FAR, recv_sem.at[S_FAR + g], to, row)
    pending.append((far.at[:, pl.ds(0, CLUSTERS - 1)], S_FAR))

    errors = []
    for g in range(GROUPS):
        wait(far.at[g, pl.ds(0, CLUSTERS - 1)], recv_sem.at[S_FAR + g])
        goal = tile(target, g, member)[...]
        below = jnp.zeros((RT, 128), F32)
        running, suffix = goal, jnp.zeros((RT, 128), F32)
        for h in range(CLUSTERS):
            total = far[g, h, 0].astype(F32)
            suffix = suffix + higher[h] * (number[h] * (goal - below) - far[g, h, 1].astype(F32))
            running = running - lower[h] * total
            below = below + total
        inclusive = []
        for j in range(MEMBERS):
            running = running - parts[g, j].astype(F32)
            inclusive.append(running)
        for j in range(MEMBERS - 1, -1, -1):
            suffix = suffix + ends_at[j] * inclusive[j]
            grads[g, j] = (-2.0 / B * suffix).astype(BF16)
        for d in Z_ORDER:
            to = lax.rem(member + d, MEMBERS)
            send(
                grads.at[g, to], tile(pgrad, g, member), S_GRAD, recv_sem.at[S_GRAD + g],
                cluster * MEMBERS + to, row,
            )
        tile(pgrad, g, member)[...] = grads[g, member]
        for k in range(PREFIXES):
            error = ends[0][k] * inclusive[0]
            for j in range(1, MEMBERS):
                error = error + ends[j][k] * inclusive[j]
            if g == 0:
                errors.append([error])
            else:
                errors[k].append(error)
    pending.append((grads.at[:, pl.ds(0, MEMBERS - 1)], S_GRAD))

    lane = lax.broadcasted_iota(jnp.int32, (1, 128), 1)
    loss_row, ended = jnp.zeros((1, 128), F32), jnp.zeros((RT, 128), F32)
    for k in range(PREFIXES):
        squares = jnp.zeros((RT, 128), F32)
        for error in errors[k]:
            squares = squares + error * error
            ended = ended + error
        square = jnp.sum(jnp.sum(squares, axis=0, keepdims=True), axis=1, keepdims=True)
        loss_row = loss_row + jnp.where(lane == k, square, 0.0)
    ended_row = -2.0 / B * jnp.sum(ended, axis=0, keepdims=True)

    down = jnp.zeros((8, LAT), F32)
    for g in range(GROUPS):
        wait(grads.at[g, pl.ds(0, MEMBERS - 1)], recv_sem.at[S_GRAD + g])
        partial = jnp.dot(pgrad[group(g)], wdec_t[...], preferred_element_type=F32)
        code_out[group(g)] = partial.astype(BF16)
        products = partial * slope[group(g)]
        for i in range(0, GR, 8):
            down = down + products[i : i + 8]
        if g == GROUPS - 1:
            benc = jnp.sum(down, axis=0, keepdims=True)
            pieces = [benc[:, 128 * k : 128 * k + 128] for k in range(LAT // 128)]
            sums[row] = jnp.concatenate(pieces + [loss_row, jnp.zeros((1, 128), F32)], axis=0)
            for xx, cc in row_peers():
                send(sums.at[row], sums.at[row], S_SUM, recv_sem.at[S_SUM], lat, xx * NC + cc)
        for xx, cc in row_peers():
            send(block(code_out, g, xx, cc), code_in.at[g, row], S_CODE, recv_sem.at[S_CODE + g], lat, xx * NC + cc)
        code_in[g, row] = block(code_out, g, x, c)[...]
    pending.append((sums.at[pl.ds(0, ROWS - 1)], S_SUM))
    pending.append((code_in.at[:, pl.ds(0, ROWS - 1)], S_CODE))

    gdec[...] = lax.dot_general(
        codes[...], pgrad[...], (((0,), (0,)), ((), ())), preferred_element_type=F32
    ).astype(BF16)
    put_dec = pltpu.make_async_copy(gdec, grad_dec, local_sem.at[L_GDEC])
    put_dec.start()

    def own_code_grad(g):
        wait(code_in.at[g, pl.ds(0, ROWS - 1)], recv_sem.at[S_CODE + g])
        code_grad = code_in[g, 0].astype(F32)
        for r in range(1, ROWS):
            code_grad = code_grad + code_in[g, r].astype(F32)
        block(pgb, g, x, c)[...] = (code_grad * sig[g]).astype(BF16)
        for xx, cc in row_peers():
            send(block(pgb, g, x, c), block(pgb, g, x, c), S_PG, recv_sem.at[S_PG], lat, xx * NC + cc)

    for g in range(GROUPS - 1):
        own_code_grad(g)

    wait(sums.at[pl.ds(0, ROWS - 1)], recv_sem.at[S_SUM])
    summed = sums[0]
    for r in range(1, ROWS):
        summed = summed + sums[r]
    benc = jnp.concatenate([summed[k : k + 1] for k in range(LAT // 128)], axis=1)
    high = benc.astype(BF16)
    middle = (benc - high.astype(F32)).astype(BF16)
    low = (benc - high.astype(F32) - middle.astype(F32)).astype(BF16)
    three = jnp.concatenate([high, middle, low, jnp.zeros((13, LAT), BF16)], axis=0)
    term = jnp.dot(three, wenc_t[...], preferred_element_type=F32)
    term = term[0:1] + (term[1:2] + term[2:3])
    pieces = [
        jnp.where(member // NY == k, ended_row, 0.0) - term[:, 128 * k : 128 * k + 128] for k in range(WIDTH // 128)
    ]
    by[y] = jnp.concatenate(pieces + [summed[6:7], jnp.zeros((3, 128), F32)], axis=0)
    for d in Y_ORDER:
        send(by.at[y], by.at[y], S_BY, recv_sem.at[S_BY], z * NY + lax.rem(y + d, NY), row)
    pending.append((by.at[pl.ds(0, NY - 1)], S_BY))
    grad_benc[...] = benc

    own_code_grad(GROUPS - 1)
    pending.append((code_in.at[:, pl.ds(0, ROWS - 1)], S_PG))

    wait(by.at[pl.ds(0, NY - 1)], recv_sem.at[S_BY])
    bz[z] = (by[0] + by[1]) + (by[2] + by[3])
    for d in Z_ORDER:
        to = lax.rem(z + d, NZ)
        send(bz.at[z], bz.at[z], S_BZ, recv_sem.at[S_BZ], to * NY + y, row)
    pending.append((bz.at[pl.ds(0, NZ - 1)], S_BZ))

    wait(code_in.at[:, pl.ds(0, ROWS - 1)], recv_sem.at[S_PG])
    genc[...] = lax.dot_general(
        centred[...], pgb[...], (((0,), (0,)), ((), ())), preferred_element_type=F32
    ).astype(BF16)
    put_enc = pltpu.make_async_copy(genc, grad_enc, local_sem.at[L_GENC])
    put_enc.start()

    for ref, sem in pending:
        wait(ref, send_sem.at[sem])
    put_dec.wait()
    put_enc.wait()
    wait(bz.at[pl.ds(0, NZ - 1)], recv_sem.at[S_BZ])
    everything = bz[0]
    for p in range(1, NZ):
        everything = everything + bz[p]
    tail[...] = everything


def finish(genc, benc, gdec, tail, grad_enc, grad_benc, grad_dec, grad_bdec, losses, sem):
    put_enc = pltpu.make_async_copy(genc, grad_enc, sem.at[0])
    put_dec = pltpu.make_async_copy(gdec, grad_dec, sem.at[1])
    put_enc.start()
    put_dec.start()
    grad_benc[...] = benc[...].reshape(LAT)
    grad_bdec[...] = tail[0:4].reshape(WIDTH)
    losses[...] = (tail[4] * (1.0 / (B * WIDTH * ROWS)))[0:PREFIXES]
    put_enc.wait()
    put_dec.wait()


def per_device(store, batch_rows, bounds, w_enc, b_enc, w_dec, b_dec):
    vmem, hbm = pl.BlockSpec(memory_space=pltpu.VMEM), pl.BlockSpec(memory_space=pl.ANY)
    operands = (store, batch_rows.reshape(1, B), bounds, w_enc, b_enc, w_dec, b_dec.reshape(1, WIDTH))
    genc, benc, gdec, tail = pl.pallas_call(
        kernel,
        out_shape=(
            jax.ShapeDtypeStruct((WIDTH, LAT), BF16),
            jax.ShapeDtypeStruct((1, LAT), F32),
            jax.ShapeDtypeStruct((LAT, WIDTH), BF16),
            jax.ShapeDtypeStruct((8, 128), F32),
        ),
        in_specs=[hbm] * 7,
        out_specs=(hbm, vmem, hbm, vmem),
        scratch_shapes=[
            pltpu.VMEM((1, B), jnp.int32),
            pltpu.SMEM((PREFIXES,), jnp.int32),
            pltpu.VMEM((LAT,), F32),
            pltpu.VMEM((1, LAT), F32),
            pltpu.VMEM((1, WIDTH), F32),
            pltpu.VMEM((WIDTH, LAT), BF16),
            pltpu.VMEM((LAT, WIDTH), BF16),
            pltpu.VMEM((LAT, WIDTH), BF16),
            pltpu.VMEM((WIDTH, LAT), BF16),
            pltpu.VMEM((B, LAT), F32),
            pltpu.VMEM((B, STORE), BF16),
            pltpu.VMEM((STORE, WIDTH), BF16),
            pltpu.VMEM((B, WIDTH), F32),
            pltpu.VMEM((B, WIDTH), BF16),
            pltpu.VMEM((B, LAT), BF16),
            pltpu.VMEM((GROUPS, ROWS, RT, CB), BF16),
            pltpu.VMEM((GROUPS, RT, CB), F32),
            pltpu.VMEM((B, LAT), BF16),
            pltpu.VMEM((B, WIDTH), BF16),
            pltpu.VMEM((GROUPS, MEMBERS, RT, 128), BF16),
            pltpu.VMEM((GROUPS, CLUSTERS, 2, RT, 128), BF16),
            pltpu.VMEM((GROUPS, MEMBERS, RT, 128), BF16),
            pltpu.VMEM((B, WIDTH), BF16),
            pltpu.VMEM((B, LAT), BF16),
            pltpu.VMEM((GROUPS, ROWS, RT, CB), BF16),
            pltpu.VMEM((B, LAT), BF16),
            pltpu.VMEM((ROWS, 8, 128), F32),
            pltpu.VMEM((LAT, WIDTH), BF16),
            pltpu.VMEM((WIDTH, LAT), BF16),
            pltpu.VMEM((NY, 8, 128), F32),
            pltpu.VMEM((NZ, 8, 128), F32),
            pltpu.SemaphoreType.DMA((9,)),
            pltpu.SemaphoreType.DMA((23,)),
            pltpu.SemaphoreType.DMA((23,)),
            pltpu.SemaphoreType.REGULAR((2,)),
        ],
        compiler_params=pltpu.CompilerParams(
            collective_id=0, has_side_effects=True, vmem_limit_bytes=40 * 2**20
        ),
        name="sae_step",
    )(*(pltpu.with_memory_space_constraint(operand, pltpu.HBM) for operand in operands))
    return pl.pallas_call(
        finish,
        out_shape=(
            jax.ShapeDtypeStruct((WIDTH, LAT), BF16),
            jax.ShapeDtypeStruct((LAT,), F32),
            jax.ShapeDtypeStruct((LAT, WIDTH), BF16),
            jax.ShapeDtypeStruct((WIDTH,), F32),
            jax.ShapeDtypeStruct((PREFIXES,), F32),
        ),
        in_specs=[hbm, vmem, hbm, vmem],
        out_specs=(hbm, vmem, hbm, vmem, vmem),
        scratch_shapes=[pltpu.SemaphoreType.DMA((2,))],
        compiler_params=pltpu.CompilerParams(vmem_limit_bytes=40 * 2**20),
        name="sae_finish",
    )(genc, benc, gdec, tail)


def solution(mesh):
    return jax.shard_map(
        per_device,
        mesh=mesh,
        in_specs=(P("row", None), P(), P(), P("row", "lat"), P("lat"), P("lat", "row"), P("row")),
        out_specs=(P("row", "lat"), P("lat"), P("lat", "row"), P("row"), P()),
        check_vma=False,
    )
```

```python
import jax
import jax.numpy as jnp
from jax import lax
from jax.experimental import pallas as pl
from jax.experimental.pallas import tpu as pltpu
from jax.sharding import PartitionSpec as P

MESH = pl.DeviceIdType.MESH
BF16, F32 = jnp.bfloat16, jnp.float32

NX, NC, NY, NZ = 4, 2, 4, 16
ROWS = NX * NC
B, STORE, PREFIXES = 192, 384, 5
WIDTH, LAT = 512, 768
SB = STORE // ROWS
GROUPS = 3
GR = B // GROUPS
RT = GR // NX
CB = LAT // NC
MEMBERS, CLUSTERS, OWNERS = 16, 4, 8
HALF = WIDTH // 2

X_ORDER = ((2, 0), (2, 1), (1, 0), (1, 1), (3, 0), (3, 1), (0, 1))
Z_ORDER = (8, 7, 9, 6, 10, 5, 11, 4, 12, 3, 13, 2, 14, 1, 15)
Y_ORDER = (2, 1, 3)
L_ORDER = sorted(
    ((dz, dy) for dz in range(NZ) for dy in range(NY) if dz or dy),
    key=lambda d: -(min(d[0], NZ - d[0]) + min(d[1], NY - d[1])),
)
O_ORDER = (6, 2, 5, 7, 1, 3, 4, 0)

L_ENC, L_DEC, L_STORE, L_GDEC, L_GENC, L_ROWS, L_BENC, L_BDEC, L_BOUNDS = range(9)
S_PRE, S_CODES, S_PART, S_FAR, S_GRAD, S_CODE = range(0, 18, 3)
S_STORE, S_PG, S_SUM, S_BIAS, S_LROW, S_LY, S_LZ = range(18, 25)


def ordered_sum(ref, count):
    total = ref[0]
    for i in range(1, count):
        total = total + ref[i]
    return total


def kernel(
    store, batch_rows_hbm, bounds_hbm, w_enc, b_enc_hbm, w_dec, b_dec_hbm,
    grad_enc, grad_benc, grad_dec, tail,
    batch_rows, bounds, b_enc_flat, b_enc, b_dec, wenc, wdec, wenc_t, wdec_t, slope, picks, cols, target, centred, pre_out, pre_in, sig, codes, part_out, parts, near, far,
    grads, losses, ended, pgrad, code_out, code_in, pgb, sums, gdec, genc, biases, by_row, by_y, by_z,
    local_sem, send_sem, recv_sem, relay_sem,
):
    lat, row = lax.axis_index("lat"), lax.axis_index("row")
    z, y = lat // NY, lax.rem(lat, NY)
    cluster, member = lat // MEMBERS, lax.rem(lat, MEMBERS)
    is_owner = jnp.logical_and(member >= NY, member < NY + OWNERS)
    own = jnp.clip(member - NY, 0, OWNERS - 1)
    x, c = row // NC, lax.rem(row, NC)

    def row_peers():
        for dx, dc in X_ORDER:
            yield lax.rem(x + dx, NX), lax.rem(c + dc, NC)

    def send(src, dst, sem, recv, lat_to, row_to):
        pltpu.make_async_remote_copy(
            src_ref=src, dst_ref=dst, send_sem=send_sem.at[sem], recv_sem=recv,
            device_id=(lat_to, row_to), device_id_type=MESH,
        ).start()

    def wait(ref, sem):
        pltpu.make_async_copy(ref, ref, sem).wait()

    def group(g):
        return pl.ds(g * GR, GR)

    def band(ref, g, i):
        return ref.at[pl.ds(pl.multiple_of(g * GR + i * RT, RT), RT)]

    def part(ref, g, owner):
        return band(ref, g, lax.rem(owner, NY)).at[:, pl.ds(pl.multiple_of(owner // NY * HALF, HALF), HALF)]

    def block(ref, g, xx, cc):
        return band(ref, g, xx).at[:, pl.ds(pl.multiple_of(cc * CB, CB), CB)]

    get_enc = pltpu.make_async_copy(w_enc, wenc, local_sem.at[L_ENC])
    get_dec = pltpu.make_async_copy(w_dec, wdec, local_sem.at[L_DEC])
    own_cols = pl.ds(pl.multiple_of(row * WIDTH, WIDTH), WIDTH)
    own_slot = pl.ds(pl.multiple_of(row * SB, SB), SB)
    get_own = pltpu.make_async_copy(store.at[:, own_cols], cols.at[own_slot], local_sem.at[L_STORE])
    get_rows = pltpu.make_async_copy(batch_rows_hbm, batch_rows, local_sem.at[L_ROWS])
    get_benc = pltpu.make_async_copy(b_enc_hbm, b_enc_flat, local_sem.at[L_BENC])
    get_bdec = pltpu.make_async_copy(b_dec_hbm, b_dec, local_sem.at[L_BDEC])
    get_bounds = pltpu.make_async_copy(bounds_hbm, bounds, local_sem.at[L_BOUNDS])
    gets = (get_own, get_rows, get_bdec, get_enc, get_benc, get_dec, get_bounds)
    for get in gets:
        get.start()
    pending = []

    barrier = pltpu.get_barrier_semaphore()
    for xx, cc in row_peers():
        pl.semaphore_signal(barrier, inc=1, device_id=(lat, xx * NC + cc), device_id_type=MESH)
    for d in range(1, NY):
        pl.semaphore_signal(barrier, inc=1, device_id=(z * NY + lax.rem(y + d, NY), row), device_id_type=MESH)
    next_z, last_z = lax.rem(z + 1, NZ) * NY + y, lax.rem(z + NZ - 1, NZ) * NY + y
    for to in (next_z, last_z):
        pl.semaphore_signal(barrier, inc=1, device_id=(to, row), device_id_type=MESH)
    pl.semaphore_wait(barrier, ROWS - 1 + NY - 1 + 2)

    def pass_on():
        pl.semaphore_signal(relay_sem.at[0], inc=1, device_id=(next_z, row), device_id_type=MESH)
        pl.semaphore_signal(relay_sem.at[1], inc=1, device_id=(last_z, row), device_id_type=MESH)

    def relay(last=False):
        pl.semaphore_wait(relay_sem.at[0], 1)
        pl.semaphore_wait(relay_sem.at[1], 1)
        if not last:
            pass_on()

    pass_on()

    for xx, cc in row_peers():
        to = xx * NC + cc
        their_cols = pl.ds(pl.multiple_of(to * WIDTH, WIDTH), WIDTH)
        send(store.at[:, their_cols], cols.at[own_slot], S_STORE, recv_sem.at[S_STORE], lat, to)
    pending.append((cols.at[pl.ds(0, SB * (ROWS - 1))], S_STORE))
    for get in gets:
        get.wait()
    b_enc[...] = b_enc_flat[...].reshape(1, LAT)
    rows_down = jnp.broadcast_to(batch_rows[...], (128, B)).T
    lanes = lax.broadcasted_iota(jnp.int32, (B, 128), 1)
    for k in range(STORE // 128):
        picks[:, 128 * k : 128 * k + 128] = (lanes + 128 * k == rows_down).astype(BF16)
    relay()
    relay()
    relay()
    wait(cols.at[pl.ds(0, SB * (ROWS - 1))], recv_sem.at[S_STORE])
    for g in range(GROUPS):
        rows = group(g)
        goal = jnp.dot(picks[rows], cols[...], preferred_element_type=F32) - b_dec[...]
        target[rows] = goal
        centred[rows] = goal.astype(BF16)
        pre_out[rows] = jnp.dot(centred[rows], wenc[...], preferred_element_type=F32).astype(BF16)
        for xx, cc in row_peers():
            send(block(pre_out, g, xx, cc), pre_in.at[g, row], S_PRE, recv_sem.at[S_PRE + g], lat, xx * NC + cc)
    pending.append((pre_in.at[:, pl.ds(0, ROWS - 1)], S_PRE))
    relay()
    relay()
    my_b_enc = b_enc[:, pl.ds(pl.multiple_of(c * CB, CB), CB)]
    for g in range(GROUPS):
        pre_in[g, row] = block(pre_out, g, x, c)[...]
        wait(pre_in.at[g, pl.ds(0, ROWS - 1)], recv_sem.at[S_PRE + g])
        preact = my_b_enc + pre_in[g, 0].astype(F32)
        for r in range(1, ROWS):
            preact = preact + pre_in[g, r].astype(F32)
        small = jnp.exp(-jnp.abs(preact))
        log1p = jnp.where(small < 1e-3, small * (1.0 - 0.5 * small), jnp.log(1.0 + small))
        block(codes, g, x, c)[...] = (jnp.maximum(preact, 0.0) + log1p).astype(BF16)
        for xx, cc in row_peers():
            send(block(codes, g, x, c), block(codes, g, x, c), S_CODES, recv_sem.at[S_CODES + g], lat, xx * NC + cc)
        sig[g] = jnp.where(preact >= 0.0, 1.0, small) / (1.0 + small)
    pending.append((pre_in.at[:, pl.ds(0, ROWS - 1)], S_CODES))

    relay()
    relay(last=True)
    for g in range(GROUPS):
        wait(pre_in.at[g, pl.ds(0, ROWS - 1)], recv_sem.at[S_CODES + g])
        part_out[group(g)] = jnp.dot(codes[group(g)], wdec[...], preferred_element_type=F32).astype(BF16)
        for d in O_ORDER:
            to = lax.rem(own + d, OWNERS)

            @pl.when(to + NY != member)
            def _():
                send(
                    part(part_out, g, to), parts.at[g, member], S_PART, recv_sem.at[S_PART + g],
                    cluster * MEMBERS + NY + to, row,
                )

    soft = codes[...].astype(F32)
    slope[...] = jnp.where(soft < 0.01, soft * (1.0 - soft * (0.5 - soft * (1.0 / 6.0))), 1.0 - jnp.exp(-soft))
    wdec_t[...] = wdec[...].T
    wenc_t[...] = wenc[...].T
    losses[...] = jnp.zeros((1, 128), F32)
    ended[...] = jnp.zeros((1, HALF), F32)

    @pl.when(is_owner)
    def _():
        ends = [
            [jnp.where(bounds[k] == cluster * MEMBERS + j + 1, 1.0, 0.0).astype(F32) for k in range(PREFIXES)]
            for j in range(MEMBERS)
        ]
        ends_at = [sum(ends[j][1:], ends[j][0]) for j in range(MEMBERS)]
        beyond = [jnp.where(bounds[k] > (cluster + 1) * MEMBERS, 1.0, 0.0).astype(F32) for k in range(PREFIXES)]
        above = sum(beyond[1:], beyond[0])

        totals = []
        for g in range(GROUPS):
            parts[g, member] = part(part_out, g, own)[...]
            wait(parts.at[g, pl.ds(0, MEMBERS - 1)], recv_sem.at[S_PART + g])
            total = parts[g, 0].astype(F32)
            cut = ends_at[0] * total
            for j in range(1, MEMBERS):
                total = total + parts[g, j].astype(F32)
                cut = cut + ends_at[j] * total
            totals.append(total)
            near[g, 0] = total.astype(BF16)
            near[g, 1] = (cut + above * total).astype(BF16)
            for d in (2, 1, 3):
                to = lax.rem(cluster + d, CLUSTERS)
                which = jnp.where(to < cluster, 1, 0)
                send(
                    near.at[g, which], far.at[g, d - 1], S_FAR, recv_sem.at[S_FAR + g],
                    to * MEMBERS + member, row,
                )

        errors = [[] for k in range(PREFIXES)]
        for g in range(GROUPS):
            wait(far.at[g], recv_sem.at[S_FAR + g])
            running = part(target, g, own)[...]
            over = jnp.zeros((RT, HALF), F32)
            for d in range(1, CLUSTERS):
                from_lower = jnp.where(d <= cluster, 1.0, 0.0).astype(F32)
                got = far[g, d - 1].astype(F32)
                running = running - from_lower * got
                over = over + (1.0 - from_lower) * got
            suffix = above * (running - totals[g]) - over
            inclusive = []
            for j in range(MEMBERS):
                running = running - parts[g, j].astype(F32)
                inclusive.append(running)
            for j in range(MEMBERS - 1, -1, -1):
                suffix = suffix + ends_at[j] * inclusive[j]
                grads[g, j] = (-2.0 / B * suffix).astype(BF16)
            for d in Z_ORDER:
                to = lax.rem(member + d, MEMBERS)
                send(
                    grads.at[g, to], part(pgrad, g, own), S_GRAD, recv_sem.at[S_GRAD + g],
                    cluster * MEMBERS + to, row,
                )
            part(pgrad, g, own)[...] = grads[g, member]
            for k in range(PREFIXES):
                error = ends[0][k] * inclusive[0]
                for j in range(1, MEMBERS):
                    error = error + ends[j][k] * inclusive[j]
                errors[k].append(error)

        lane = lax.broadcasted_iota(jnp.int32, (1, 128), 1)
        loss_row, all_errors = jnp.zeros((1, 128), F32), jnp.zeros((RT, HALF), F32)
        for k in range(PREFIXES):
            squares = jnp.zeros((RT, HALF), F32)
            for error in errors[k]:
                squares = squares + error * error
                all_errors = all_errors + error
            square = jnp.sum(jnp.sum(squares, axis=0, keepdims=True), axis=1, keepdims=True)
            loss_row = loss_row + jnp.where(lane == k, square, 0.0)
        losses[...] = loss_row
        ended[...] = -2.0 / B * jnp.sum(all_errors, axis=0, keepdims=True)

    by_row[row] = losses[...]
    for xx, cc in row_peers():
        send(by_row.at[row], by_row.at[row], S_LROW, recv_sem.at[S_LROW], lat, xx * NC + cc)
    pending.append((by_row.at[pl.ds(0, ROWS - 1)], S_LROW))

    down = jnp.zeros((8, LAT), F32)
    for g in range(GROUPS):

        @pl.when(is_owner)
        def _():
            wait(grads.at[g, pl.ds(0, OWNERS - 1)], recv_sem.at[S_GRAD + g])

        @pl.when(jnp.logical_not(is_owner))
        def _():
            wait(grads.at[g, pl.ds(0, OWNERS)], recv_sem.at[S_GRAD + g])

        partial = jnp.dot(pgrad[group(g)], wdec_t[...], preferred_element_type=F32)
        code_out[group(g)] = partial.astype(BF16)
        products = partial * slope[group(g)]
        for i in range(0, GR, 8):
            down = down + products[i : i + 8]
        if g == GROUPS - 1:
            benc = jnp.sum(down, axis=0, keepdims=True)
            pieces = [benc[:, 128 * k : 128 * k + 128] for k in range(LAT // 128)]
            sums[row] = jnp.concatenate(pieces + [jnp.zeros((2, 128), F32)], axis=0)
            for xx, cc in row_peers():
                send(sums.at[row], sums.at[row], S_SUM, recv_sem.at[S_SUM], lat, xx * NC + cc)
        for xx, cc in row_peers():
            send(block(code_out, g, xx, cc), code_in.at[g, row], S_CODE, recv_sem.at[S_CODE + g], lat, xx * NC + cc)
        code_in[g, row] = block(code_out, g, x, c)[...]
        if g == 0:
            wait(by_row.at[pl.ds(0, ROWS - 1)], recv_sem.at[S_LROW])
            by_y[y] = ordered_sum(by_row, ROWS)
            for d in Y_ORDER:
                send(by_y.at[y], by_y.at[y], S_LY, recv_sem.at[S_LY], z * NY + lax.rem(y + d, NY), row)
            pending.append((by_y.at[pl.ds(0, NY - 1)], S_LY))
    pending.append((sums.at[pl.ds(0, ROWS - 1)], S_SUM))
    pending.append((code_in.at[:, pl.ds(0, ROWS - 1)], S_CODE))

    gdec[...] = lax.dot_general(
        codes[...], pgrad[...], (((0,), (0,)), ((), ())), preferred_element_type=F32
    ).astype(BF16)
    put_dec = pltpu.make_async_copy(gdec, grad_dec, local_sem.at[L_GDEC])
    put_dec.start()

    def own_code_grad(g):
        wait(code_in.at[g, pl.ds(0, ROWS - 1)], recv_sem.at[S_CODE + g])
        code_grad = code_in[g, 0].astype(F32)
        for r in range(1, ROWS):
            code_grad = code_grad + code_in[g, r].astype(F32)
        block(pgb, g, x, c)[...] = (code_grad * sig[g]).astype(BF16)
        for xx, cc in row_peers():
            send(block(pgb, g, x, c), block(pgb, g, x, c), S_PG, recv_sem.at[S_PG], lat, xx * NC + cc)

    wait(by_y.at[pl.ds(0, NY - 1)], recv_sem.at[S_LY])
    by_z[z] = ordered_sum(by_y, NY)
    for d in Z_ORDER:
        send(by_z.at[z], by_z.at[z], S_LZ, recv_sem.at[S_LZ], lax.rem(z + d, NZ) * NY + y, row)
    pending.append((by_z.at[pl.ds(0, NZ - 1)], S_LZ))
    for g in range(GROUPS - 1):
        own_code_grad(g)

    wait(sums.at[pl.ds(0, ROWS - 1)], recv_sem.at[S_SUM])
    summed = ordered_sum(sums, ROWS)
    benc = jnp.concatenate([summed[k : k + 1] for k in range(LAT // 128)], axis=1)
    high = benc.astype(BF16)
    middle = (benc - high.astype(F32)).astype(BF16)
    low = (benc - high.astype(F32) - middle.astype(F32)).astype(BF16)
    three = jnp.concatenate([high, middle, low, jnp.zeros((13, LAT), BF16)], axis=0)
    term = jnp.dot(three, wenc_t[...], preferred_element_type=F32)
    term = term[0:1] + (term[1:2] + term[2:3])
    bias = jnp.concatenate([jnp.where(own // NY == k, ended[...], 0.0) for k in range(2)], axis=1) - term
    pieces = [bias[:, 128 * k : 128 * k + 128] for k in range(WIDTH // 128)]
    biases[lat, 0:4] = jnp.concatenate(pieces, axis=0)
    for dz, dy in L_ORDER:
        to = lax.rem(z + dz, NZ) * NY + lax.rem(y + dy, NY)
        mine = biases.at[lat, pl.ds(0, 4)]
        send(mine, mine, S_BIAS, recv_sem.at[S_BIAS], to, row)
    pending.append((biases.at[pl.ds(0, NY * NZ - 1), pl.ds(0, 4)], S_BIAS))
    grad_benc[...] = benc

    own_code_grad(GROUPS - 1)
    pending.append((code_in.at[:, pl.ds(0, ROWS - 1)], S_PG))

    wait(code_in.at[:, pl.ds(0, ROWS - 1)], recv_sem.at[S_PG])
    genc[...] = lax.dot_general(
        centred[...], pgb[...], (((0,), (0,)), ((), ())), preferred_element_type=F32
    ).astype(BF16)
    put_enc = pltpu.make_async_copy(genc, grad_enc, local_sem.at[L_GENC])
    put_enc.start()

    @pl.when(is_owner)
    def _():
        wait(parts.at[:, pl.ds(0, OWNERS - 1)], send_sem.at[S_PART])
        wait(far, send_sem.at[S_FAR])
        wait(grads.at[:, pl.ds(0, MEMBERS - 1)], send_sem.at[S_GRAD])

    @pl.when(jnp.logical_not(is_owner))
    def _():
        wait(parts.at[:, pl.ds(0, OWNERS)], send_sem.at[S_PART])

    for ref, sem in pending:
        wait(ref, send_sem.at[sem])
    put_dec.wait()
    put_enc.wait()
    wait(by_z.at[pl.ds(0, NZ - 1)], recv_sem.at[S_LZ])
    tail[4:5] = ordered_sum(by_z, NZ)
    wait(biases.at[pl.ds(0, NY * NZ - 1), pl.ds(0, 4)], recv_sem.at[S_BIAS])
    quarters = []
    for first in range(0, NY * NZ, NZ):
        quarter = biases[first, 0:4]
        for i in range(first + 1, first + NZ):
            quarter = quarter + biases[i, 0:4]
        quarters.append(quarter)
    tail[0:4] = (quarters[0] + quarters[1]) + (quarters[2] + quarters[3])


def finish(genc, benc, gdec, tail, *refs):
    (outs, flat, sem) = (refs[:5], refs[5:8], refs[8])
    sources = (genc, flat[0], gdec, flat[1], flat[2])
    puts = [pltpu.make_async_copy(sources[i], outs[i], sem.at[i]) for i in range(5)]
    puts[0].start()
    puts[2].start()
    flat[0][...] = benc[...].reshape(LAT)
    flat[1][...] = tail[0:4].reshape(WIDTH)
    flat[2][...] = (tail[4] * (1.0 / (B * WIDTH * ROWS)))[0:PREFIXES]
    for i in (1, 3, 4):
        puts[i].start()
    for put in puts:
        put.wait()


def per_device(store, batch_rows, bounds, w_enc, b_enc, w_dec, b_dec):
    vmem, hbm = pl.BlockSpec(memory_space=pltpu.VMEM), pl.BlockSpec(memory_space=pl.ANY)
    operands = (store, batch_rows.reshape(1, B), bounds, w_enc, b_enc, w_dec, b_dec.reshape(1, WIDTH))
    genc, benc, gdec, tail = pl.pallas_call(
        kernel,
        out_shape=(
            jax.ShapeDtypeStruct((WIDTH, LAT), BF16),
            jax.ShapeDtypeStruct((1, LAT), F32),
            jax.ShapeDtypeStruct((LAT, WIDTH), BF16),
            jax.ShapeDtypeStruct((8, 128), F32),
        ),
        in_specs=[hbm] * 7,
        out_specs=(hbm, vmem, hbm, vmem),
        scratch_shapes=[
            pltpu.VMEM((1, B), jnp.int32),
            pltpu.SMEM((PREFIXES,), jnp.int32),
            pltpu.VMEM((LAT,), F32),
            pltpu.VMEM((1, LAT), F32),
            pltpu.VMEM((1, WIDTH), F32),
            pltpu.VMEM((WIDTH, LAT), BF16),
            pltpu.VMEM((LAT, WIDTH), BF16),
            pltpu.VMEM((LAT, WIDTH), BF16),
            pltpu.VMEM((WIDTH, LAT), BF16),
            pltpu.VMEM((B, LAT), F32),
            pltpu.VMEM((B, STORE), BF16),
            pltpu.VMEM((STORE, WIDTH), BF16),
            pltpu.VMEM((B, WIDTH), F32),
            pltpu.VMEM((B, WIDTH), BF16),
            pltpu.VMEM((B, LAT), BF16),
            pltpu.VMEM((GROUPS, ROWS, RT, CB), BF16),
            pltpu.VMEM((GROUPS, RT, CB), F32),
            pltpu.VMEM((B, LAT), BF16),
            pltpu.VMEM((B, WIDTH), BF16),
            pltpu.VMEM((GROUPS, MEMBERS, RT, HALF), BF16),
            pltpu.VMEM((GROUPS, 2, RT, HALF), BF16),
            pltpu.VMEM((GROUPS, CLUSTERS - 1, RT, HALF), BF16),
            pltpu.VMEM((GROUPS, MEMBERS, RT, HALF), BF16),
            pltpu.VMEM((1, 128), F32),
            pltpu.VMEM((1, HALF), F32),
            pltpu.VMEM((B, WIDTH), BF16),
            pltpu.VMEM((B, LAT), BF16),
            pltpu.VMEM((GROUPS, ROWS, RT, CB), BF16),
            pltpu.VMEM((B, LAT), BF16),
            pltpu.VMEM((ROWS, 8, 128), F32),
            pltpu.VMEM((LAT, WIDTH), BF16),
            pltpu.VMEM((WIDTH, LAT), BF16),
            pltpu.VMEM((NY * NZ, 8, 128), F32),
            pltpu.VMEM((ROWS, 1, 128), F32),
            pltpu.VMEM((NY, 1, 128), F32),
            pltpu.VMEM((NZ, 1, 128), F32),
            pltpu.SemaphoreType.DMA((9,)),
            pltpu.SemaphoreType.DMA((25,)),
            pltpu.SemaphoreType.DMA((25,)),
            pltpu.SemaphoreType.REGULAR((2,)),
        ],
        compiler_params=pltpu.CompilerParams(
            collective_id=0, has_side_effects=True, vmem_limit_bytes=40 * 2**20
        ),
        name="sae_step",
    )(*(pltpu.with_memory_space_constraint(operand, pltpu.HBM) for operand in operands))
    return pl.pallas_call(
        finish,
        out_shape=(
            jax.ShapeDtypeStruct((WIDTH, LAT), BF16),
            jax.ShapeDtypeStruct((LAT,), F32),
            jax.ShapeDtypeStruct((LAT, WIDTH), BF16),
            jax.ShapeDtypeStruct((WIDTH,), F32),
            jax.ShapeDtypeStruct((PREFIXES,), F32),
        ),
        in_specs=[hbm, vmem, hbm, vmem],
        out_specs=[hbm] * 5,
        scratch_shapes=[
            pltpu.VMEM((LAT,), F32),
            pltpu.VMEM((WIDTH,), F32),
            pltpu.VMEM((PREFIXES,), F32),
            pltpu.SemaphoreType.DMA((5,)),
        ],
        compiler_params=pltpu.CompilerParams(vmem_limit_bytes=40 * 2**20),
        name="sae_finish",
    )(genc, benc, gdec, tail)


def solution(mesh):
    return jax.shard_map(
        per_device,
        mesh=mesh,
        in_specs=(P("row", None), P(), P(), P("row", "lat"), P("lat"), P("lat", "row"), P("row")),
        out_specs=(P("row", "lat"), P("lat"), P("lat", "row"), P("row"), P()),
        check_vma=False,
    )
```

```python
import jax
import jax.numpy as jnp
from jax import lax
from jax.experimental import pallas as pl
from jax.experimental.pallas import tpu as pltpu
from jax.sharding import PartitionSpec as P

MESH = pl.DeviceIdType.MESH
BF16, F32 = jnp.bfloat16, jnp.float32

NX, NC, NY, NZ = 4, 2, 4, 16
ROWS = NX * NC
B, STORE, PREFIXES = 192, 384, 5
WIDTH, LAT = 512, 768
SB = STORE // ROWS
GROUPS = 3
GR = B // GROUPS
RT = GR // NX
CB = LAT // NC
MEMBERS, CLUSTERS, OWNERS = 16, 4, 8
HALF = WIDTH // 2

X_ORDER = ((2, 0), (2, 1), (1, 0), (1, 1), (3, 0), (3, 1), (0, 1))
Z_ORDER = (8, 7, 9, 6, 10, 5, 11, 4, 12, 3, 13, 2, 14, 1, 15)
Y_ORDER = (2, 1, 3)
L_ORDER = sorted(
    ((dz, dy) for dz in range(NZ) for dy in range(NY) if dz or dy),
    key=lambda d: -(min(d[0], NZ - d[0]) + min(d[1], NY - d[1])),
)
O_ORDER = (2, 1, 3, 0, 6, 5, 7, 4)

L_ENC, L_DEC, L_STORE, L_GDEC, L_GENC, L_ROWS, L_BENC, L_BDEC, L_BOUNDS, L_GBENC, L_TAIL = range(11)
S_PRE, S_CODES, S_PART, S_FAR, S_GRAD, S_CODE = range(0, 18, 3)
S_STORE, S_PG, S_SUM, S_BIAS, S_LROW, S_LY, S_LZ = range(18, 25)


def ordered_sum(ref, count):
    total = ref[0]
    for i in range(1, count):
        total = total + ref[i]
    return total


def kernel(
    store_hbm, batch_rows_hbm, bounds_hbm, w_enc, b_enc_hbm, w_dec, b_dec_hbm,
    grad_enc, grad_benc_out, grad_dec, tail_out,
    grad_benc, tail,    store, batch_rows, bounds, b_enc_flat, b_enc, b_dec, wenc, wdec, wenc_t, wdec_t, slope, picks, cols, target, centred, pre_out, pre_in, sig, codes, part_out, parts, near, far,
    grads, losses, ended, pgrad, code_out, code_in, pgb, sums, gdec, genc, biases, by_row, by_y, by_z,
    local_sem, send_sem, recv_sem, relay_sem,
):
    lat, row = lax.axis_index("lat"), lax.axis_index("row")
    z, y = lat // NY, lax.rem(lat, NY)
    cluster, member = lat // MEMBERS, lax.rem(lat, MEMBERS)
    is_owner = jnp.logical_and(member >= NY, member < NY + OWNERS)
    own = jnp.clip(member - NY, 0, OWNERS - 1)
    x, c = row // NC, lax.rem(row, NC)

    def row_peers():
        for dx, dc in X_ORDER:
            yield lax.rem(x + dx, NX), lax.rem(c + dc, NC)

    def send(src, dst, sem, recv, lat_to, row_to):
        pltpu.make_async_remote_copy(
            src_ref=src, dst_ref=dst, send_sem=send_sem.at[sem], recv_sem=recv,
            device_id=(lat_to, row_to), device_id_type=MESH,
        ).start()

    def wait(ref, sem):
        pltpu.make_async_copy(ref, ref, sem).wait()

    def group(g):
        return pl.ds(g * GR, GR)

    def band(ref, g, i):
        return ref.at[pl.ds(pl.multiple_of(g * GR + i * RT, RT), RT)]

    def part(ref, g, owner):
        return band(ref, g, lax.rem(owner, NY)).at[:, pl.ds(pl.multiple_of(owner // NY * HALF, HALF), HALF)]

    def block(ref, g, xx, cc):
        return band(ref, g, xx).at[:, pl.ds(pl.multiple_of(cc * CB, CB), CB)]

    get_enc = pltpu.make_async_copy(w_enc, wenc, local_sem.at[L_ENC])
    get_dec = pltpu.make_async_copy(w_dec, wdec, local_sem.at[L_DEC])
    own_slot = pl.ds(pl.multiple_of(row * SB, SB), SB)
    get_own = pltpu.make_async_copy(store_hbm, store, local_sem.at[L_STORE])
    get_rows = pltpu.make_async_copy(batch_rows_hbm, batch_rows, local_sem.at[L_ROWS])
    get_benc = pltpu.make_async_copy(b_enc_hbm, b_enc_flat, local_sem.at[L_BENC])
    get_bdec = pltpu.make_async_copy(b_dec_hbm, b_dec, local_sem.at[L_BDEC])
    get_bounds = pltpu.make_async_copy(bounds_hbm, bounds, local_sem.at[L_BOUNDS])
    gets = (get_own, get_rows, get_bdec, get_enc, get_benc, get_dec, get_bounds)
    for get in gets:
        get.start()
    pending = []

    barrier = pltpu.get_barrier_semaphore()
    for xx, cc in row_peers():
        pl.semaphore_signal(barrier, inc=1, device_id=(lat, xx * NC + cc), device_id_type=MESH)
    for d in range(1, NY):
        pl.semaphore_signal(barrier, inc=1, device_id=(z * NY + lax.rem(y + d, NY), row), device_id_type=MESH)
    next_z, last_z = lax.rem(z + 1, NZ) * NY + y, lax.rem(z + NZ - 1, NZ) * NY + y
    for to in (next_z, last_z):
        pl.semaphore_signal(barrier, inc=1, device_id=(to, row), device_id_type=MESH)
    pl.semaphore_wait(barrier, ROWS - 1 + NY - 1 + 2)

    def pass_on():
        pl.semaphore_signal(relay_sem.at[0], inc=1, device_id=(next_z, row), device_id_type=MESH)
        pl.semaphore_signal(relay_sem.at[1], inc=1, device_id=(last_z, row), device_id_type=MESH)

    def relay(last=False):
        pl.semaphore_wait(relay_sem.at[0], 1)
        pl.semaphore_wait(relay_sem.at[1], 1)
        if not last:
            pass_on()

    pass_on()

    get_own.wait()
    for xx, cc in row_peers():
        to = xx * NC + cc
        their_cols = pl.ds(pl.multiple_of(to * WIDTH, WIDTH), WIDTH)
        send(store.at[:, their_cols], cols.at[own_slot], S_STORE, recv_sem.at[S_STORE], lat, to)
    pending.append((cols.at[pl.ds(0, SB * (ROWS - 1))], S_STORE))
    cols[own_slot] = store[:, pl.ds(pl.multiple_of(row * WIDTH, WIDTH), WIDTH)]
    for get in gets[1:]:
        get.wait()
    b_enc[...] = b_enc_flat[...].reshape(1, LAT)
    rows_down = jnp.broadcast_to(batch_rows[...], (128, B)).T
    lanes = lax.broadcasted_iota(jnp.int32, (B, 128), 1)
    for k in range(STORE // 128):
        picks[:, 128 * k : 128 * k + 128] = (lanes + 128 * k == rows_down).astype(BF16)
    relay()
    relay()
    relay()
    wait(cols.at[pl.ds(0, SB * (ROWS - 1))], recv_sem.at[S_STORE])
    for g in range(GROUPS):
        rows = group(g)
        goal = jnp.dot(picks[rows], cols[...], preferred_element_type=F32) - b_dec[...]
        target[rows] = goal
        centred[rows] = goal.astype(BF16)
        pre_out[rows] = jnp.dot(centred[rows], wenc[...], preferred_element_type=F32).astype(BF16)
        for xx, cc in row_peers():
            send(block(pre_out, g, xx, cc), pre_in.at[g, row], S_PRE, recv_sem.at[S_PRE + g], lat, xx * NC + cc)
    pending.append((pre_in.at[:, pl.ds(0, ROWS - 1)], S_PRE))
    relay()
    relay()
    my_b_enc = b_enc[:, pl.ds(pl.multiple_of(c * CB, CB), CB)]
    for g in range(GROUPS):
        pre_in[g, row] = block(pre_out, g, x, c)[...]
        wait(pre_in.at[g, pl.ds(0, ROWS - 1)], recv_sem.at[S_PRE + g])
        preact = my_b_enc + pre_in[g, 0].astype(F32)
        for r in range(1, ROWS):
            preact = preact + pre_in[g, r].astype(F32)
        small = jnp.exp(-jnp.abs(preact))
        log1p = jnp.where(small < 1e-3, small * (1.0 - 0.5 * small), jnp.log(1.0 + small))
        block(codes, g, x, c)[...] = (jnp.maximum(preact, 0.0) + log1p).astype(BF16)
        for xx, cc in row_peers():
            send(block(codes, g, x, c), block(codes, g, x, c), S_CODES, recv_sem.at[S_CODES + g], lat, xx * NC + cc)
        if g < 2:
            relay(last=g == 1)
        sig[g] = jnp.where(preact >= 0.0, 1.0, small) / (1.0 + small)
    pending.append((pre_in.at[:, pl.ds(0, ROWS - 1)], S_CODES))

    for g in range(GROUPS):
        wait(pre_in.at[g, pl.ds(0, ROWS - 1)], recv_sem.at[S_CODES + g])
        part_out[group(g)] = jnp.dot(codes[group(g)], wdec[...], preferred_element_type=F32).astype(BF16)
        for d in O_ORDER:
            to = lax.rem(lax.rem(member, NY) + d, NY) + NY * lax.rem(jnp.where(member < 2 * NY, 1, 0) + d // NY, 2)

            @pl.when(to + NY != member)
            def _():
                send(
                    part(part_out, g, to), parts.at[g, member], S_PART, recv_sem.at[S_PART + g],
                    cluster * MEMBERS + NY + to, row,
                )

    soft = codes[...].astype(F32)
    slope[...] = jnp.where(soft < 0.01, soft * (1.0 - soft * (0.5 - soft * (1.0 / 6.0))), 1.0 - jnp.exp(-soft))
    wdec_t[...] = wdec[...].T
    wenc_t[...] = wenc[...].T
    losses[...] = jnp.zeros((1, 128), F32)
    ended[...] = jnp.zeros((1, HALF), F32)

    @pl.when(is_owner)
    def _():
        ends = [
            [jnp.where(bounds[k] == cluster * MEMBERS + j + 1, 1.0, 0.0).astype(F32) for k in range(PREFIXES)]
            for j in range(MEMBERS)
        ]
        ends_at = [sum(ends[j][1:], ends[j][0]) for j in range(MEMBERS)]
        beyond = [jnp.where(bounds[k] > (cluster + 1) * MEMBERS, 1.0, 0.0).astype(F32) for k in range(PREFIXES)]
        above = sum(beyond[1:], beyond[0])

        totals = []
        for g in range(GROUPS):
            parts[g, member] = part(part_out, g, own)[...]
            wait(parts.at[g, pl.ds(0, MEMBERS - 1)], recv_sem.at[S_PART + g])
            total = parts[g, 0].astype(F32)
            cut = ends_at[0] * total
            for j in range(1, MEMBERS):
                total = total + parts[g, j].astype(F32)
                cut = cut + ends_at[j] * total
            totals.append(total)
            near[g, 0] = total.astype(BF16)
            near[g, 1] = (cut + above * total).astype(BF16)
            for d in (2, 1, 3):
                to = lax.rem(cluster + d, CLUSTERS)
                which = jnp.where(to < cluster, 1, 0)
                send(
                    near.at[g, which], far.at[g, d - 1], S_FAR, recv_sem.at[S_FAR + g],
                    to * MEMBERS + member, row,
                )

        errors = [[] for k in range(PREFIXES)]
        for g in range(GROUPS):
            wait(far.at[g], recv_sem.at[S_FAR + g])
            running = part(target, g, own)[...]
            over = jnp.zeros((RT, HALF), F32)
            for d in range(1, CLUSTERS):
                from_lower = jnp.where(d <= cluster, 1.0, 0.0).astype(F32)
                got = far[g, d - 1].astype(F32)
                running = running - from_lower * got
                over = over + (1.0 - from_lower) * got
            suffix = above * (running - totals[g]) - over
            inclusive = []
            for j in range(MEMBERS):
                running = running - parts[g, j].astype(F32)
                inclusive.append(running)
            for j in range(MEMBERS - 1, -1, -1):
                suffix = suffix + ends_at[j] * inclusive[j]
                grads[g, j] = (-2.0 / B * suffix).astype(BF16)
            for plane in (3, 0, 2, 1):
                for d in (Y_ORDER if plane == 1 else Y_ORDER + (0,)):
                    to = NY * jnp.where(member < 2 * NY, plane, 3 - plane) + lax.rem(member + d, NY)
                    send(
                        grads.at[g, to], part(pgrad, g, own), S_GRAD, recv_sem.at[S_GRAD + g],
                        cluster * MEMBERS + to, row,
                    )
            part(pgrad, g, own)[...] = grads[g, member]
            for k in range(PREFIXES):
                error = ends[0][k] * inclusive[0]
                for j in range(1, MEMBERS):
                    error = error + ends[j][k] * inclusive[j]
                errors[k].append(error)

        lane = lax.broadcasted_iota(jnp.int32, (1, 128), 1)
        loss_row, all_errors = jnp.zeros((1, 128), F32), jnp.zeros((RT, HALF), F32)
        for k in range(PREFIXES):
            squares = jnp.zeros((RT, HALF), F32)
            for error in errors[k]:
                squares = squares + error * error
                all_errors = all_errors + error
            square = jnp.sum(jnp.sum(squares, axis=0, keepdims=True), axis=1, keepdims=True)
            loss_row = loss_row + jnp.where(lane == k, square, 0.0)
        losses[...] = loss_row
        ended[...] = -2.0 / B * jnp.sum(all_errors, axis=0, keepdims=True)

    by_row[row] = losses[...]
    for xx, cc in row_peers():
        send(by_row.at[row], by_row.at[row], S_LROW, recv_sem.at[S_LROW], lat, xx * NC + cc)
    pending.append((by_row.at[pl.ds(0, ROWS - 1)], S_LROW))

    down = jnp.zeros((8, LAT), F32)
    for g in range(GROUPS):

        @pl.when(is_owner)
        def _():
            wait(grads.at[g, pl.ds(0, OWNERS - 1)], recv_sem.at[S_GRAD + g])

        @pl.when(jnp.logical_not(is_owner))
        def _():
            wait(grads.at[g, pl.ds(0, OWNERS)], recv_sem.at[S_GRAD + g])

        partial = jnp.dot(pgrad[group(g)], wdec_t[...], preferred_element_type=F32)
        products = partial * slope[group(g)]
        for i in range(0, GR, 8):
            down = down + products[i : i + 8]
        if g == GROUPS - 1:
            benc = jnp.sum(down, axis=0, keepdims=True)
            pieces = [benc[:, 128 * k : 128 * k + 128] for k in range(LAT // 128)]
            sums[row] = jnp.concatenate(pieces + [jnp.zeros((2, 128), F32)], axis=0)
            for xx, cc in row_peers():
                send(sums.at[row], sums.at[row], S_SUM, recv_sem.at[S_SUM], lat, xx * NC + cc)
        code_out[group(g)] = partial.astype(BF16)
        for xx, cc in row_peers():
            send(block(code_out, g, xx, cc), code_in.at[g, row], S_CODE, recv_sem.at[S_CODE + g], lat, xx * NC + cc)
        code_in[g, row] = block(code_out, g, x, c)[...]
        if g == 0:
            wait(by_row.at[pl.ds(0, ROWS - 1)], recv_sem.at[S_LROW])
            by_y[y] = ordered_sum(by_row, ROWS)
            for d in Y_ORDER:
                send(by_y.at[y], by_y.at[y], S_LY, recv_sem.at[S_LY], z * NY + lax.rem(y + d, NY), row)
            pending.append((by_y.at[pl.ds(0, NY - 1)], S_LY))
    pending.append((sums.at[pl.ds(0, ROWS - 1)], S_SUM))
    pending.append((code_in.at[:, pl.ds(0, ROWS - 1)], S_CODE))

    gdec[...] = lax.dot_general(
        codes[...], pgrad[...], (((0,), (0,)), ((), ())), preferred_element_type=F32
    ).astype(BF16)

    def own_code_grad(g):
        wait(code_in.at[g, pl.ds(0, ROWS - 1)], recv_sem.at[S_CODE + g])
        code_grad = code_in[g, 0].astype(F32)
        for r in range(1, ROWS):
            code_grad = code_grad + code_in[g, r].astype(F32)
        block(pgb, g, x, c)[...] = (code_grad * sig[g]).astype(BF16)
        for xx, cc in row_peers():
            send(block(pgb, g, x, c), block(pgb, g, x, c), S_PG, recv_sem.at[S_PG], lat, xx * NC + cc)

    wait(by_y.at[pl.ds(0, NY - 1)], recv_sem.at[S_LY])
    by_z[z] = ordered_sum(by_y, NY)
    for d in Z_ORDER:
        send(by_z.at[z], by_z.at[z], S_LZ, recv_sem.at[S_LZ], lax.rem(z + d, NZ) * NY + y, row)
    pending.append((by_z.at[pl.ds(0, NZ - 1)], S_LZ))
    for g in range(GROUPS - 1):
        own_code_grad(g)

    wait(sums.at[pl.ds(0, ROWS - 1)], recv_sem.at[S_SUM])
    summed = ordered_sum(sums, ROWS)
    benc = jnp.concatenate([summed[k : k + 1] for k in range(LAT // 128)], axis=1)
    high = benc.astype(BF16)
    middle = (benc - high.astype(F32)).astype(BF16)
    low = (benc - high.astype(F32) - middle.astype(F32)).astype(BF16)
    three = jnp.concatenate([high, middle, low, jnp.zeros((13, LAT), BF16)], axis=0)
    term = jnp.dot(three, wenc_t[...], preferred_element_type=F32)
    term = term[0:1] + (term[1:2] + term[2:3])
    bias = jnp.concatenate([jnp.where(own // NY == k, ended[...], 0.0) for k in range(2)], axis=1) - term
    pieces = [bias[:, 128 * k : 128 * k + 128] for k in range(WIDTH // 128)]
    biases[lat, 0:4] = jnp.concatenate(pieces, axis=0)
    for dz, dy in L_ORDER:
        to = lax.rem(z + dz, NZ) * NY + lax.rem(y + dy, NY)
        mine = biases.at[lat, pl.ds(0, 4)]
        send(mine, mine, S_BIAS, recv_sem.at[S_BIAS], to, row)
    pending.append((biases.at[pl.ds(0, NY * NZ - 1), pl.ds(0, 4)], S_BIAS))
    grad_benc[...] = benc
    put_benc = pltpu.make_async_copy(grad_benc, grad_benc_out, local_sem.at[L_GBENC])
    put_benc.start()
    put_dec = pltpu.make_async_copy(gdec, grad_dec, local_sem.at[L_GDEC])
    put_dec.start()

    own_code_grad(GROUPS - 1)
    pending.append((code_in.at[:, pl.ds(0, ROWS - 1)], S_PG))

    wait(code_in.at[:, pl.ds(0, ROWS - 1)], recv_sem.at[S_PG])
    genc[...] = lax.dot_general(
        centred[...], pgb[...], (((0,), (0,)), ((), ())), preferred_element_type=F32
    ).astype(BF16)
    put_enc = pltpu.make_async_copy(genc, grad_enc, local_sem.at[L_GENC])
    put_enc.start()

    @pl.when(is_owner)
    def _():
        wait(parts.at[:, pl.ds(0, OWNERS - 1)], send_sem.at[S_PART])
        wait(far, send_sem.at[S_FAR])
        wait(grads.at[:, pl.ds(0, MEMBERS - 1)], send_sem.at[S_GRAD])

    @pl.when(jnp.logical_not(is_owner))
    def _():
        wait(parts.at[:, pl.ds(0, OWNERS)], send_sem.at[S_PART])

    for ref, sem in pending:
        wait(ref, send_sem.at[sem])
    put_dec.wait()
    put_enc.wait()
    wait(by_z.at[pl.ds(0, NZ - 1)], recv_sem.at[S_LZ])
    tail[4:8] = jnp.broadcast_to(ordered_sum(by_z, NZ), (4, 128))
    wait(biases.at[pl.ds(0, NY * NZ - 1), pl.ds(0, 4)], recv_sem.at[S_BIAS])
    quarters = []
    for first in range(0, NY * NZ, NZ):
        quarter = biases[first, 0:4]
        for i in range(first + 1, first + NZ):
            quarter = quarter + biases[i, 0:4]
        quarters.append(quarter)
    tail[0:4] = (quarters[0] + quarters[1]) + (quarters[2] + quarters[3])
    put_tail = pltpu.make_async_copy(tail, tail_out, local_sem.at[L_TAIL])
    put_tail.start()
    put_benc.wait()
    put_tail.wait()


def finish(genc, benc, gdec, tail, *refs):
    (outs, flat, sem) = (refs[:5], refs[5:8], refs[8])
    sources = (genc, flat[0], gdec, flat[1], flat[2])
    puts = [pltpu.make_async_copy(sources[i], outs[i], sem.at[i]) for i in range(5)]
    puts[0].start()
    puts[2].start()
    flat[0][...] = benc[...].reshape(LAT)
    flat[1][...] = tail[0:4].reshape(WIDTH)
    flat[2][...] = (tail[4] * (1.0 / (B * WIDTH * ROWS)))[0:PREFIXES]
    for i in (1, 3, 4):
        puts[i].start()
    for put in puts:
        put.wait()


def per_device(store, batch_rows, bounds, w_enc, b_enc, w_dec, b_dec):
    vmem, hbm = pl.BlockSpec(memory_space=pltpu.VMEM), pl.BlockSpec(memory_space=pl.ANY)
    operands = (store, batch_rows.reshape(1, B), bounds, w_enc, b_enc, w_dec, b_dec.reshape(1, WIDTH))
    genc, benc, gdec, tail = pl.pallas_call(
        kernel,
        out_shape=(
            jax.ShapeDtypeStruct((WIDTH, LAT), BF16),
            jax.ShapeDtypeStruct((1, LAT), F32),
            jax.ShapeDtypeStruct((LAT, WIDTH), BF16),
            jax.ShapeDtypeStruct((8, 128), F32),
        ),
        in_specs=[hbm] * 7,
        out_specs=[hbm] * 4,
        scratch_shapes=[
            pltpu.VMEM((1, LAT), F32),
            pltpu.VMEM((8, 128), F32),
            pltpu.VMEM((SB, WIDTH * ROWS), BF16),
            pltpu.VMEM((1, B), jnp.int32),
            pltpu.SMEM((PREFIXES,), jnp.int32),
            pltpu.VMEM((LAT,), F32),
            pltpu.VMEM((1, LAT), F32),
            pltpu.VMEM((1, WIDTH), F32),
            pltpu.VMEM((WIDTH, LAT), BF16),
            pltpu.VMEM((LAT, WIDTH), BF16),
            pltpu.VMEM((LAT, WIDTH), BF16),
            pltpu.VMEM((WIDTH, LAT), BF16),
            pltpu.VMEM((B, LAT), F32),
            pltpu.VMEM((B, STORE), BF16),
            pltpu.VMEM((STORE, WIDTH), BF16),
            pltpu.VMEM((B, WIDTH), F32),
            pltpu.VMEM((B, WIDTH), BF16),
            pltpu.VMEM((B, LAT), BF16),
            pltpu.VMEM((GROUPS, ROWS, RT, CB), BF16),
            pltpu.VMEM((GROUPS, RT, CB), F32),
            pltpu.VMEM((B, LAT), BF16),
            pltpu.VMEM((B, WIDTH), BF16),
            pltpu.VMEM((GROUPS, MEMBERS, RT, HALF), BF16),
            pltpu.VMEM((GROUPS, 2, RT, HALF), BF16),
            pltpu.VMEM((GROUPS, CLUSTERS - 1, RT, HALF), BF16),
            pltpu.VMEM((GROUPS, MEMBERS, RT, HALF), BF16),
            pltpu.VMEM((1, 128), F32),
            pltpu.VMEM((1, HALF), F32),
            pltpu.VMEM((B, WIDTH), BF16),
            pltpu.VMEM((B, LAT), BF16),
            pltpu.VMEM((GROUPS, ROWS, RT, CB), BF16),
            pltpu.VMEM((B, LAT), BF16),
            pltpu.VMEM((ROWS, 8, 128), F32),
            pltpu.VMEM((LAT, WIDTH), BF16),
            pltpu.VMEM((WIDTH, LAT), BF16),
            pltpu.VMEM((NY * NZ, 8, 128), F32),
            pltpu.VMEM((ROWS, 1, 128), F32),
            pltpu.VMEM((NY, 1, 128), F32),
            pltpu.VMEM((NZ, 1, 128), F32),
            pltpu.SemaphoreType.DMA((11,)),
            pltpu.SemaphoreType.DMA((25,)),
            pltpu.SemaphoreType.DMA((25,)),
            pltpu.SemaphoreType.REGULAR((2,)),
        ],
        compiler_params=pltpu.CompilerParams(
            collective_id=0, has_side_effects=True, vmem_limit_bytes=40 * 2**20
        ),
        name="sae_step",
    )(*(pltpu.with_memory_space_constraint(operand, pltpu.HBM) for operand in operands))
    return pl.pallas_call(
        finish,
        out_shape=(
            jax.ShapeDtypeStruct((WIDTH, LAT), BF16),
            jax.ShapeDtypeStruct((LAT,), F32),
            jax.ShapeDtypeStruct((LAT, WIDTH), BF16),
            jax.ShapeDtypeStruct((WIDTH,), F32),
            jax.ShapeDtypeStruct((PREFIXES,), F32),
        ),
        in_specs=[hbm, vmem, hbm, vmem],
        out_specs=[hbm] * 5,
        scratch_shapes=[
            pltpu.VMEM((LAT,), F32),
            pltpu.VMEM((WIDTH,), F32),
            pltpu.VMEM((PREFIXES,), F32),
            pltpu.SemaphoreType.DMA((5,)),
        ],
        compiler_params=pltpu.CompilerParams(vmem_limit_bytes=40 * 2**20),
        name="sae_finish",
    )(genc, benc, gdec, tail)


def solution(mesh):
    return jax.shard_map(
        per_device,
        mesh=mesh,
        in_specs=(P("row", None), P(), P(), P("row", "lat"), P("lat"), P("lat", "row"), P("row")),
        out_specs=(P("row", "lat"), P("lat"), P("lat", "row"), P("row"), P()),
        check_vma=False,
    )
```

```python
import jax
import jax.numpy as jnp
from jax import lax
from jax.experimental import pallas as pl
from jax.experimental.pallas import tpu as pltpu
from jax.sharding import PartitionSpec as P

MESH = pl.DeviceIdType.MESH
BF16, F32 = jnp.bfloat16, jnp.float32

NX, NC, NY, NZ = 4, 2, 4, 16
ROWS = NX * NC
B, STORE, PREFIXES = 192, 384, 5
WIDTH, LAT = 512, 768
SB = STORE // ROWS
GROUPS = 3
GR = B // GROUPS
RT = GR // NX
CB = LAT // NC
MEMBERS, CLUSTERS, OWNERS = 16, 4, 8
HALF = WIDTH // 2

X_ORDER = ((2, 0), (2, 1), (1, 0), (3, 0), (1, 1), (3, 1), (0, 1))
Z_ORDER = (8, 7, 9, 6, 10, 5, 11, 4, 12, 3, 13, 2, 14, 1, 15)
Y_ORDER = (2, 1, 3)
L_ORDER = sorted(
    ((dz, dy) for dz in range(NZ) for dy in range(NY) if dz or dy),
    key=lambda d: -(min(d[0], NZ - d[0]) + min(d[1], NY - d[1])),
)
O_ORDER = (2, 1, 3, 0, 6, 5, 7, 4)

L_ENC, L_DEC, L_STORE, L_GDEC, L_GENC, L_ROWS, L_BENC, L_BDEC, L_BOUNDS, L_GBENC, L_TAIL = range(11)
S_PRE, S_CODES, S_PART, S_FAR, S_GRAD, S_CODE = range(0, 18, 3)
S_STORE, S_PG, S_SUM, S_BIAS, S_LROW, S_LY, S_LZ = range(18, 25)


def ordered_sum(ref, count):
    total = ref[0]
    for i in range(1, count):
        total = total + ref[i]
    return total


def kernel(
    store_hbm, batch_rows_hbm, bounds_hbm, w_enc, b_enc_hbm, w_dec, b_dec_hbm,
    grad_enc, grad_benc_out, grad_dec, tail_out,
    grad_benc, tail,    store, batch_rows, bounds, b_enc_flat, b_enc, b_dec, wenc, wdec, wenc_t, wdec_t, slope, picks, cols, target, centred, pre_out, pre_in, sig, codes, part_out, parts, near, far,
    grads, losses, ended, pgrad, code_out, code_in, pgb, sums, gdec, genc, biases, by_row, by_y, by_z,
    local_sem, send_sem, recv_sem, relay_sem,
):
    lat, row = lax.axis_index("lat"), lax.axis_index("row")
    z, y = lat // NY, lax.rem(lat, NY)
    cluster, member = lat // MEMBERS, lax.rem(lat, MEMBERS)
    is_owner = jnp.logical_and(member >= NY, member < NY + OWNERS)
    own = jnp.clip(member - NY, 0, OWNERS - 1)
    x, c = row // NC, lax.rem(row, NC)

    def row_peers():
        for dx, dc in X_ORDER:
            yield lax.rem(x + dx, NX), lax.rem(c + dc, NC)

    def send(src, dst, sem, recv, lat_to, row_to):
        pltpu.make_async_remote_copy(
            src_ref=src, dst_ref=dst, send_sem=send_sem.at[sem], recv_sem=recv,
            device_id=(lat_to, row_to), device_id_type=MESH,
        ).start()

    def wait(ref, sem):
        pltpu.make_async_copy(ref, ref, sem).wait()

    def group(g):
        return pl.ds(g * GR, GR)

    def band(ref, g, i):
        return ref.at[pl.ds(pl.multiple_of(g * GR + i * RT, RT), RT)]

    def part(ref, g, owner):
        return band(ref, g, lax.rem(owner, NY)).at[:, pl.ds(pl.multiple_of(owner // NY * HALF, HALF), HALF)]

    def block(ref, g, xx, cc):
        return band(ref, g, xx).at[:, pl.ds(pl.multiple_of(cc * CB, CB), CB)]

    get_enc = pltpu.make_async_copy(w_enc, wenc, local_sem.at[L_ENC])
    get_dec = pltpu.make_async_copy(w_dec, wdec, local_sem.at[L_DEC])
    own_slot = pl.ds(pl.multiple_of(row * SB, SB), SB)
    get_own = pltpu.make_async_copy(store_hbm, store, local_sem.at[L_STORE])
    get_rows = pltpu.make_async_copy(batch_rows_hbm, batch_rows, local_sem.at[L_ROWS])
    get_benc = pltpu.make_async_copy(b_enc_hbm, b_enc_flat, local_sem.at[L_BENC])
    get_bdec = pltpu.make_async_copy(b_dec_hbm, b_dec, local_sem.at[L_BDEC])
    get_bounds = pltpu.make_async_copy(bounds_hbm, bounds, local_sem.at[L_BOUNDS])
    gets = (get_own, get_rows, get_bdec, get_enc, get_benc, get_dec, get_bounds)
    for get in gets:
        get.start()
    pending = []

    barrier = pltpu.get_barrier_semaphore()
    for xx, cc in row_peers():
        pl.semaphore_signal(barrier, inc=1, device_id=(lat, xx * NC + cc), device_id_type=MESH)
    for d in range(1, NY):
        pl.semaphore_signal(barrier, inc=1, device_id=(z * NY + lax.rem(y + d, NY), row), device_id_type=MESH)
    next_z, last_z = lax.rem(z + 1, NZ) * NY + y, lax.rem(z + NZ - 1, NZ) * NY + y
    for to in (next_z, last_z):
        pl.semaphore_signal(barrier, inc=1, device_id=(to, row), device_id_type=MESH)
    pl.semaphore_wait(barrier, ROWS - 1 + NY - 1 + 2)

    def pass_on():
        pl.semaphore_signal(relay_sem.at[0], inc=1, device_id=(next_z, row), device_id_type=MESH)
        pl.semaphore_signal(relay_sem.at[1], inc=1, device_id=(last_z, row), device_id_type=MESH)

    def relay(last=False):
        pl.semaphore_wait(relay_sem.at[0], 1)
        pl.semaphore_wait(relay_sem.at[1], 1)
        if not last:
            pass_on()

    pass_on()

    get_own.wait()
    for xx, cc in row_peers():
        to = xx * NC + cc
        their_cols = pl.ds(pl.multiple_of(to * WIDTH, WIDTH), WIDTH)
        send(store.at[:, their_cols], cols.at[own_slot], S_STORE, recv_sem.at[S_STORE], lat, to)
    pending.append((cols.at[pl.ds(0, SB * (ROWS - 1))], S_STORE))
    cols[own_slot] = store[:, pl.ds(pl.multiple_of(row * WIDTH, WIDTH), WIDTH)]
    for get in gets[1:]:
        get.wait()
    b_enc[...] = b_enc_flat[...].reshape(1, LAT)
    rows_down = jnp.broadcast_to(batch_rows[...], (128, B)).T
    lanes = lax.broadcasted_iota(jnp.int32, (B, 128), 1)
    for k in range(STORE // 128):
        picks[:, 128 * k : 128 * k + 128] = (lanes + 128 * k == rows_down).astype(BF16)
    relay()
    relay()
    relay()
    wait(cols.at[pl.ds(0, SB * (ROWS - 1))], recv_sem.at[S_STORE])
    for g in range(GROUPS):
        rows = group(g)
        goal = jnp.dot(picks[rows], cols[...], preferred_element_type=F32) - b_dec[...]
        target[rows] = goal
        centred[rows] = goal.astype(BF16)
        pre_out[rows] = jnp.dot(centred[rows], wenc[...], preferred_element_type=F32).astype(BF16)
        for xx, cc in row_peers():
            send(block(pre_out, g, xx, cc), pre_in.at[g, row], S_PRE, recv_sem.at[S_PRE + g], lat, xx * NC + cc)
    pending.append((pre_in.at[:, pl.ds(0, ROWS - 1)], S_PRE))
    relay()
    relay()
    my_b_enc = b_enc[:, pl.ds(pl.multiple_of(c * CB, CB), CB)]
    for g in range(GROUPS):
        pre_in[g, row] = block(pre_out, g, x, c)[...]
        wait(pre_in.at[g, pl.ds(0, ROWS - 1)], recv_sem.at[S_PRE + g])
        preact = my_b_enc + pre_in[g, 0].astype(F32)
        for r in range(1, ROWS):
            preact = preact + pre_in[g, r].astype(F32)
        small = jnp.exp(-jnp.abs(preact))
        log1p = jnp.where(small < 1e-3, small * (1.0 - 0.5 * small), jnp.log(1.0 + small))
        block(codes, g, x, c)[...] = (jnp.maximum(preact, 0.0) + log1p).astype(BF16)
        for xx, cc in row_peers():
            send(block(codes, g, x, c), block(codes, g, x, c), S_CODES, recv_sem.at[S_CODES + g], lat, xx * NC + cc)
        if g < 2:
            relay(last=g == 1)
        sig[g] = jnp.where(preact >= 0.0, 1.0, small) / (1.0 + small)
    pending.append((pre_in.at[:, pl.ds(0, ROWS - 1)], S_CODES))

    for g in range(GROUPS):
        wait(pre_in.at[g, pl.ds(0, ROWS - 1)], recv_sem.at[S_CODES + g])
        part_out[group(g)] = jnp.dot(codes[group(g)], wdec[...], preferred_element_type=F32).astype(BF16)
        for d in O_ORDER:
            to = lax.rem(lax.rem(member, NY) + d, NY) + NY * lax.rem(jnp.where(member < 2 * NY, 1, 0) + d // NY, 2)

            @pl.when(to + NY != member)
            def _():
                send(
                    part(part_out, g, to), parts.at[g, member], S_PART, recv_sem.at[S_PART + g],
                    cluster * MEMBERS + NY + to, row,
                )

    soft = codes[...].astype(F32)
    slope[...] = jnp.where(soft < 0.01, soft * (1.0 - soft * (0.5 - soft * (1.0 / 6.0))), 1.0 - jnp.exp(-soft))
    wdec_t[...] = wdec[...].T
    wenc_t[...] = wenc[...].T
    losses[...] = jnp.zeros((1, 128), F32)
    ended[...] = jnp.zeros((1, HALF), F32)

    @pl.when(is_owner)
    def _():
        ends = [
            [jnp.where(bounds[k] == cluster * MEMBERS + j + 1, 1.0, 0.0).astype(F32) for k in range(PREFIXES)]
            for j in range(MEMBERS)
        ]
        ends_at = [sum(ends[j][1:], ends[j][0]) for j in range(MEMBERS)]
        beyond = [jnp.where(bounds[k] > (cluster + 1) * MEMBERS, 1.0, 0.0).astype(F32) for k in range(PREFIXES)]
        above = sum(beyond[1:], beyond[0])

        totals = []
        for g in range(GROUPS):
            parts[g, member] = part(part_out, g, own)[...]
            wait(parts.at[g, pl.ds(0, MEMBERS - 1)], recv_sem.at[S_PART + g])
            total = parts[g, 0].astype(F32)
            cut = ends_at[0] * total
            for j in range(1, MEMBERS):
                total = total + parts[g, j].astype(F32)
                cut = cut + ends_at[j] * total
            totals.append(total)
            near[g, 0] = total.astype(BF16)
            near[g, 1] = (cut + above * total).astype(BF16)
            for d in (2, 1, 3):
                to = lax.rem(cluster + d, CLUSTERS)
                which = jnp.where(to < cluster, 1, 0)
                send(
                    near.at[g, which], far.at[g, d - 1], S_FAR, recv_sem.at[S_FAR + g],
                    to * MEMBERS + member, row,
                )

        errors = [[] for k in range(PREFIXES)]
        for g in range(GROUPS):
            wait(far.at[g], recv_sem.at[S_FAR + g])
            running = part(target, g, own)[...]
            over = jnp.zeros((RT, HALF), F32)
            for d in range(1, CLUSTERS):
                from_lower = jnp.where(d <= cluster, 1.0, 0.0).astype(F32)
                got = far[g, d - 1].astype(F32)
                running = running - from_lower * got
                over = over + (1.0 - from_lower) * got
            suffix = above * (running - totals[g]) - over
            inclusive = []
            for j in range(MEMBERS):
                running = running - parts[g, j].astype(F32)
                inclusive.append(running)
            for j in range(MEMBERS - 1, -1, -1):
                suffix = suffix + ends_at[j] * inclusive[j]
                grads[g, j] = (-2.0 / B * suffix).astype(BF16)
            for plane in (3, 0, 2, 1):
                for d in (Y_ORDER if plane == 1 else Y_ORDER + (0,)):
                    to = NY * jnp.where(member < 2 * NY, plane, 3 - plane) + lax.rem(member + d, NY)
                    send(
                        grads.at[g, to], part(pgrad, g, own), S_GRAD, recv_sem.at[S_GRAD + g],
                        cluster * MEMBERS + to, row,
                    )
            part(pgrad, g, own)[...] = grads[g, member]
            for k in range(PREFIXES):
                error = ends[0][k] * inclusive[0]
                for j in range(1, MEMBERS):
                    error = error + ends[j][k] * inclusive[j]
                errors[k].append(error)

        lane = lax.broadcasted_iota(jnp.int32, (1, 128), 1)
        loss_row, all_errors = jnp.zeros((1, 128), F32), jnp.zeros((RT, HALF), F32)
        for k in range(PREFIXES):
            squares = jnp.zeros((RT, HALF), F32)
            for error in errors[k]:
                squares = squares + error * error
                all_errors = all_errors + error
            square = jnp.sum(jnp.sum(squares, axis=0, keepdims=True), axis=1, keepdims=True)
            loss_row = loss_row + jnp.where(lane == k, square, 0.0)
        losses[...] = loss_row
        ended[...] = -2.0 / B * jnp.sum(all_errors, axis=0, keepdims=True)

    by_row[row] = losses[...]
    for xx, cc in row_peers():
        send(by_row.at[row], by_row.at[row], S_LROW, recv_sem.at[S_LROW], lat, xx * NC + cc)
    pending.append((by_row.at[pl.ds(0, ROWS - 1)], S_LROW))

    down = jnp.zeros((8, LAT), F32)
    for g in range(GROUPS):

        @pl.when(is_owner)
        def _():
            wait(grads.at[g, pl.ds(0, OWNERS - 1)], recv_sem.at[S_GRAD + g])

        @pl.when(jnp.logical_not(is_owner))
        def _():
            wait(grads.at[g, pl.ds(0, OWNERS)], recv_sem.at[S_GRAD + g])

        partial = jnp.dot(pgrad[group(g)], wdec_t[...], preferred_element_type=F32)
        products = partial * slope[group(g)]
        for i in range(0, GR, 8):
            down = down + products[i : i + 8]
        if g == GROUPS - 1:
            benc = jnp.sum(down, axis=0, keepdims=True)
            pieces = [benc[:, 128 * k : 128 * k + 128] for k in range(LAT // 128)]
            sums[row] = jnp.concatenate(pieces + [jnp.zeros((2, 128), F32)], axis=0)
            for xx, cc in row_peers():
                send(sums.at[row], sums.at[row], S_SUM, recv_sem.at[S_SUM], lat, xx * NC + cc)
        code_out[group(g)] = partial.astype(BF16)
        for xx, cc in row_peers():
            send(block(code_out, g, xx, cc), code_in.at[g, row], S_CODE, recv_sem.at[S_CODE + g], lat, xx * NC + cc)
        code_in[g, row] = block(code_out, g, x, c)[...]
        if g == 0:
            wait(by_row.at[pl.ds(0, ROWS - 1)], recv_sem.at[S_LROW])
            by_y[y] = ordered_sum(by_row, ROWS)
            for d in Y_ORDER:
                send(by_y.at[y], by_y.at[y], S_LY, recv_sem.at[S_LY], z * NY + lax.rem(y + d, NY), row)
            pending.append((by_y.at[pl.ds(0, NY - 1)], S_LY))
    pending.append((sums.at[pl.ds(0, ROWS - 1)], S_SUM))
    pending.append((code_in.at[:, pl.ds(0, ROWS - 1)], S_CODE))

    gdec[...] = lax.dot_general(
        codes[...], pgrad[...], (((0,), (0,)), ((), ())), preferred_element_type=F32
    ).astype(BF16)

    def own_code_grad(g):
        wait(code_in.at[g, pl.ds(0, ROWS - 1)], recv_sem.at[S_CODE + g])
        code_grad = code_in[g, 0].astype(F32)
        for r in range(1, ROWS):
            code_grad = code_grad + code_in[g, r].astype(F32)
        block(pgb, g, x, c)[...] = (code_grad * sig[g]).astype(BF16)
        for xx, cc in row_peers():
            send(block(pgb, g, x, c), block(pgb, g, x, c), S_PG, recv_sem.at[S_PG], lat, xx * NC + cc)

    wait(by_y.at[pl.ds(0, NY - 1)], recv_sem.at[S_LY])
    by_z[z] = ordered_sum(by_y, NY)
    for d in Z_ORDER:
        send(by_z.at[z], by_z.at[z], S_LZ, recv_sem.at[S_LZ], lax.rem(z + d, NZ) * NY + y, row)
    pending.append((by_z.at[pl.ds(0, NZ - 1)], S_LZ))
    for g in range(GROUPS - 1):
        own_code_grad(g)

    wait(sums.at[pl.ds(0, ROWS - 1)], recv_sem.at[S_SUM])
    summed = ordered_sum(sums, ROWS)
    benc = jnp.concatenate([summed[k : k + 1] for k in range(LAT // 128)], axis=1)
    high = benc.astype(BF16)
    middle = (benc - high.astype(F32)).astype(BF16)
    low = (benc - high.astype(F32) - middle.astype(F32)).astype(BF16)
    three = jnp.concatenate([high, middle, low, jnp.zeros((13, LAT), BF16)], axis=0)
    term = jnp.dot(three, wenc_t[...], preferred_element_type=F32)
    term = term[0:1] + (term[1:2] + term[2:3])
    bias = jnp.concatenate([jnp.where(own // NY == k, ended[...], 0.0) for k in range(2)], axis=1) - term
    pieces = [bias[:, 128 * k : 128 * k + 128] for k in range(WIDTH // 128)]
    biases[lat, 0:4] = jnp.concatenate(pieces, axis=0)
    for dz, dy in L_ORDER:
        to = lax.rem(z + dz, NZ) * NY + lax.rem(y + dy, NY)
        mine = biases.at[lat, pl.ds(0, 4)]
        send(mine, mine, S_BIAS, recv_sem.at[S_BIAS], to, row)
    pending.append((biases.at[pl.ds(0, NY * NZ - 1), pl.ds(0, 4)], S_BIAS))
    grad_benc[...] = benc
    put_benc = pltpu.make_async_copy(grad_benc, grad_benc_out, local_sem.at[L_GBENC])
    put_benc.start()
    put_dec = pltpu.make_async_copy(gdec, grad_dec, local_sem.at[L_GDEC])
    put_dec.start()

    own_code_grad(GROUPS - 1)
    pending.append((code_in.at[:, pl.ds(0, ROWS - 1)], S_PG))

    wait(code_in.at[:, pl.ds(0, ROWS - 1)], recv_sem.at[S_PG])
    genc[...] = lax.dot_general(
        centred[...], pgb[...], (((0,), (0,)), ((), ())), preferred_element_type=F32
    ).astype(BF16)
    put_enc = pltpu.make_async_copy(genc, grad_enc, local_sem.at[L_GENC])
    put_enc.start()

    @pl.when(is_owner)
    def _():
        wait(parts.at[:, pl.ds(0, OWNERS - 1)], send_sem.at[S_PART])
        wait(far, send_sem.at[S_FAR])
        wait(grads.at[:, pl.ds(0, MEMBERS - 1)], send_sem.at[S_GRAD])

    @pl.when(jnp.logical_not(is_owner))
    def _():
        wait(parts.at[:, pl.ds(0, OWNERS)], send_sem.at[S_PART])

    for ref, sem in pending:
        wait(ref, send_sem.at[sem])
    put_dec.wait()
    put_enc.wait()
    wait(by_z.at[pl.ds(0, NZ - 1)], recv_sem.at[S_LZ])
    tail[4:8] = jnp.broadcast_to(ordered_sum(by_z, NZ), (4, 128))
    wait(biases.at[pl.ds(0, NY * NZ - 1), pl.ds(0, 4)], recv_sem.at[S_BIAS])
    quarters = []
    for first in range(0, NY * NZ, NZ):
        quarter = biases[first, 0:4]
        for i in range(first + 1, first + NZ):
            quarter = quarter + biases[i, 0:4]
        quarters.append(quarter)
    tail[0:4] = (quarters[0] + quarters[1]) + (quarters[2] + quarters[3])
    put_tail = pltpu.make_async_copy(tail, tail_out, local_sem.at[L_TAIL])
    put_tail.start()
    put_benc.wait()
    put_tail.wait()


def finish(genc, benc, gdec, tail, *refs):
    (outs, flat, sem) = (refs[:5], refs[5:8], refs[8])
    sources = (genc, flat[0], gdec, flat[1], flat[2])
    puts = [pltpu.make_async_copy(sources[i], outs[i], sem.at[i]) for i in range(5)]
    puts[0].start()
    puts[2].start()
    flat[0][...] = benc[...].reshape(LAT)
    flat[1][...] = tail[0:4].reshape(WIDTH)
    flat[2][...] = (tail[4] * (1.0 / (B * WIDTH * ROWS)))[0:PREFIXES]
    for i in (1, 3, 4):
        puts[i].start()
    for put in puts:
        put.wait()


def per_device(store, batch_rows, bounds, w_enc, b_enc, w_dec, b_dec):
    vmem, hbm = pl.BlockSpec(memory_space=pltpu.VMEM), pl.BlockSpec(memory_space=pl.ANY)
    operands = (store, batch_rows.reshape(1, B), bounds, w_enc, b_enc, w_dec, b_dec.reshape(1, WIDTH))
    genc, benc, gdec, tail = pl.pallas_call(
        kernel,
        out_shape=(
            jax.ShapeDtypeStruct((WIDTH, LAT), BF16),
            jax.ShapeDtypeStruct((1, LAT), F32),
            jax.ShapeDtypeStruct((LAT, WIDTH), BF16),
            jax.ShapeDtypeStruct((8, 128), F32),
        ),
        in_specs=[hbm] * 7,
        out_specs=[hbm] * 4,
        scratch_shapes=[
            pltpu.VMEM((1, LAT), F32),
            pltpu.VMEM((8, 128), F32),
            pltpu.VMEM((SB, WIDTH * ROWS), BF16),
            pltpu.VMEM((1, B), jnp.int32),
            pltpu.SMEM((PREFIXES,), jnp.int32),
            pltpu.VMEM((LAT,), F32),
            pltpu.VMEM((1, LAT), F32),
            pltpu.VMEM((1, WIDTH), F32),
            pltpu.VMEM((WIDTH, LAT), BF16),
            pltpu.VMEM((LAT, WIDTH), BF16),
            pltpu.VMEM((LAT, WIDTH), BF16),
            pltpu.VMEM((WIDTH, LAT), BF16),
            pltpu.VMEM((B, LAT), F32),
            pltpu.VMEM((B, STORE), BF16),
            pltpu.VMEM((STORE, WIDTH), BF16),
            pltpu.VMEM((B, WIDTH), F32),
            pltpu.VMEM((B, WIDTH), BF16),
            pltpu.VMEM((B, LAT), BF16),
            pltpu.VMEM((GROUPS, ROWS, RT, CB), BF16),
            pltpu.VMEM((GROUPS, RT, CB), F32),
            pltpu.VMEM((B, LAT), BF16),
            pltpu.VMEM((B, WIDTH), BF16),
            pltpu.VMEM((GROUPS, MEMBERS, RT, HALF), BF16),
            pltpu.VMEM((GROUPS, 2, RT, HALF), BF16),
            pltpu.VMEM((GROUPS, CLUSTERS - 1, RT, HALF), BF16),
            pltpu.VMEM((GROUPS, MEMBERS, RT, HALF), BF16),
            pltpu.VMEM((1, 128), F32),
            pltpu.VMEM((1, HALF), F32),
            pltpu.VMEM((B, WIDTH), BF16),
            pltpu.VMEM((B, LAT), BF16),
            pltpu.VMEM((GROUPS, ROWS, RT, CB), BF16),
            pltpu.VMEM((B, LAT), BF16),
            pltpu.VMEM((ROWS, 8, 128), F32),
            pltpu.VMEM((LAT, WIDTH), BF16),
            pltpu.VMEM((WIDTH, LAT), BF16),
            pltpu.VMEM((NY * NZ, 8, 128), F32),
            pltpu.VMEM((ROWS, 1, 128), F32),
            pltpu.VMEM((NY, 1, 128), F32),
            pltpu.VMEM((NZ, 1, 128), F32),
            pltpu.SemaphoreType.DMA((11,)),
            pltpu.SemaphoreType.DMA((25,)),
            pltpu.SemaphoreType.DMA((25,)),
            pltpu.SemaphoreType.REGULAR((2,)),
        ],
        compiler_params=pltpu.CompilerParams(
            collective_id=0, has_side_effects=True, vmem_limit_bytes=40 * 2**20
        ),
        name="sae_step",
    )(*(pltpu.with_memory_space_constraint(operand, pltpu.HBM) for operand in operands))
    return pl.pallas_call(
        finish,
        out_shape=(
            jax.ShapeDtypeStruct((WIDTH, LAT), BF16),
            jax.ShapeDtypeStruct((LAT,), F32),
            jax.ShapeDtypeStruct((LAT, WIDTH), BF16),
            jax.ShapeDtypeStruct((WIDTH,), F32),
            jax.ShapeDtypeStruct((PREFIXES,), F32),
        ),
        in_specs=[hbm, vmem, hbm, vmem],
        out_specs=[hbm] * 5,
        scratch_shapes=[
            pltpu.VMEM((LAT,), F32),
            pltpu.VMEM((WIDTH,), F32),
            pltpu.VMEM((PREFIXES,), F32),
            pltpu.SemaphoreType.DMA((5,)),
        ],
        compiler_params=pltpu.CompilerParams(vmem_limit_bytes=40 * 2**20),
        name="sae_finish",
    )(genc, benc, gdec, tail)


def solution(mesh):
    return jax.shard_map(
        per_device,
        mesh=mesh,
        in_specs=(P("row", None), P(), P(), P("row", "lat"), P("lat"), P("lat", "row"), P("row")),
        out_specs=(P("row", "lat"), P("lat"), P("lat", "row"), P("row"), P()),
        check_vma=False,
    )
```
